256 devices in a mesh: row: 16 (over z, core), dev: 16 (over x, y).
Axes of the slice: x: 4, y: 4, z: 8, core: 2. Of those that a mesh axis runs over, the one named last changes fastest.
Arguments:
- primary: bfloat16 [3, 64, 262144], P(None, None, ('row', 'dev')), may hold values from -6 to 6
- conductivity: bfloat16 [64, 262144], P(None, ('row', 'dev')), may hold values from 0.19921875 to 2
- anchor_x: int32 [16, 16], P('row'), may hold values from 0 to 464
- owner: int32 [16, 16], P('row'), may hold values from 0 to 15, as said below
- gate_index: int32 [30], replicated, may hold values from 0 to 63
- misfit: float32 [16, 16, 30], P('row'), may hold values from -1.2 to 1.2
Outputs:
- gradient: float32 [64, 262144], P(None, ('row', 'dev'))
- adjoint_field: float32 [512, 3, 40, 2304], P(('row', 'dev'))
The draws below stay inside these ranges and needn't reach their ends.
Inputs may be any that keep to these rules, and one draw needn't show every extreme that they name: `owner`: in every block no device owns more than 2 footprints, and some device owns exactly 2.
All inputs are finite; a program needn't handle non-finite values.
Results may differ from the reference program's by a relative error of at most 0.0003.
Values may be sent and summed in bfloat16 or wider, within the bound.
No kernel may reach another device: no remote copies, remote signals or barrier semaphores. Data moves between devices by JAX's collectives and lax.ppermute only.
A program may use at most 128 MiB of HBM per device.

```python
import math
import jax
import jax.numpy as jnp
from jax import lax

TX = 32
TY = 32
GZ = 64
FZ = 40
FP = 48
GATES = 30
NTIMES = 64
STEPS = 2
MOST = 2
FOOT_ROW = 16
HALO = 8
GX = 512
GY = 512
GCOLS = 262144
SLOTS = 512
N_ROW = 16
N_DEV = 16


def owners_of_block(key):
    first, second, third = jax.random.split(key, 3)
    total = N_DEV * MOST
    full = jax.random.randint(first, (), 0, N_DEV)
    order = jax.random.permutation(second, total)
    places = jnp.zeros((total,), jnp.int32).at[order].set(jnp.arange(total, dtype=jnp.int32))
    slots = jnp.arange(total, dtype=jnp.int32)
    priority = jnp.where(slots // MOST == full, slots % MOST - MOST, places)
    chosen = jnp.argsort(priority, stable=True)[:FOOT_ROW]
    owners = (chosen // MOST).astype(jnp.int32)
    return owners[jax.random.permutation(third, FOOT_ROW)]


def draw_owner(key, part):
    keys = jax.random.split(jax.random.fold_in(key, 17), N_ROW)
    return jax.vmap(owners_of_block)(keys).astype(jnp.int32)


def place_ends(array, own_key, low, high):
    index_at = [jax.random.randint(jax.random.fold_in(own_key, axis), (), 0, length) for axis, length in enumerate(array.shape)]
    longest = array.shape.index(max(array.shape))
    next_to = index_at[:longest] + [(index_at[longest] + 1) % array.shape[longest]] + index_at[longest + 1:]
    return array.at[tuple(index_at)].set(low).at[tuple(next_to)].set(high)


def steps_of(stream_key, shape, cuts, smallest, largest):
    gain, own = 1.0, jax.random.fold_in(stream_key, 6)
    for dim, blocks in cuts:
        heights = jnp.exp(jax.random.uniform(jax.random.fold_in(own, dim), (blocks,), jnp.float32, smallest / len(cuts), largest / len(cuts)))
        gain = gain * jnp.repeat(heights, shape[dim] // blocks).reshape([-1 if axis == dim else 1 for axis in range(len(shape))])
    return gain


def scatter_about(rng, dims, scale, bound, shards=(), kind=jnp.bfloat16):
    result = scale * jax.random.normal(rng, dims, jnp.float32)
    if shards:
        result = result * steps_of(rng, dims, shards, -0.22, 0.18)
    return jnp.clip(result, -bound, bound).astype(kind)


def setup_inputs(seed: int = 0) -> dict:
    seeds = jax.random.split(jax.random.key(seed), 7)
    primary = scatter_about(seeds[0], (3, GZ, GCOLS), 1.0, 6.0, ((2, 256),))
    conductivity = jnp.clip(jnp.exp(math.log(2.0) - 2.306499 * jax.random.uniform(seeds[1], (GZ, GCOLS), jnp.float32) ** steps_of(seeds[1], (GZ, GCOLS), ((1, 256),), -0.2, 0.2)), 0.19921875, 2.0).astype(jnp.bfloat16)
    anchor_x = place_ends(jax.random.randint(seeds[2], (N_ROW, FOOT_ROW), 0, TX * N_DEV - FP + 1), jax.random.fold_in(seeds[2], 1), 0, TX * N_DEV - FP).astype(jnp.int32)
    owner = draw_owner(jax.random.fold_in(seeds[6], 71), 0)
    gate_index = place_ends(jax.random.randint(seeds[4], (GATES,), 0, NTIMES), jax.random.fold_in(seeds[4], 1), 0, NTIMES - 1).astype(jnp.int32)
    misfit = scatter_about(seeds[5], (N_ROW, FOOT_ROW, GATES), 0.2, 1.2, ((0, 16),), jnp.float32)
    return {"primary": primary, "conductivity": conductivity, "anchor_x": anchor_x, "owner": owner, "gate_index": gate_index, "misfit": misfit}


step_size = 0.05


def forward_diff(field, axis):
    size = field.shape[axis]
    ahead = jnp.concatenate([lax.slice_in_dim(field, 1, size, axis=axis), jnp.zeros_like(lax.slice_in_dim(field, 0, 1, axis=axis))], axis)
    return ahead - field


def adjoint_diff(field, axis):
    size = field.shape[axis]
    behind = jnp.concatenate([jnp.zeros_like(lax.slice_in_dim(field, 0, 1, axis=axis)), lax.slice_in_dim(field, 0, size - 1, axis=axis)], axis)
    return behind - field


def curl_curl(lam):
    vx, vy, vz = lam[0], lam[1], lam[2]
    wx = forward_diff(vz, 1) - forward_diff(vy, 0)
    wy = forward_diff(vx, 0) - forward_diff(vz, 2)
    wz = forward_diff(vy, 2) - forward_diff(vx, 1)
    ux = adjoint_diff(wy, 0) - adjoint_diff(wz, 1)
    uy = adjoint_diff(wz, 2) - adjoint_diff(wx, 0)
    uz = adjoint_diff(wx, 1) - adjoint_diff(wy, 2)
    return jnp.stack([ux, uy, uz], 0)


def footprint(window, residues, times):
    field = window[:3]
    sigma = window[3]

    def add_gate(g, acc):
        return acc + residues[g] * jnp.exp(-sigma * times[g])

    weight = lax.fori_loop(0, GATES, add_gate, jnp.zeros_like(sigma))
    lam = weight[None] * field
    for step in range(STEPS):
        lam = lam - step_size * (curl_curl(lam) + sigma[None] * lam)
    local = jnp.sum(lam * field, axis=0)
    return lam, local


def regularize(conductivity):
    logs = jnp.log(conductivity.astype(jnp.float32))
    delta = logs[1:] - logs[:-1]
    zero_row = jnp.zeros_like(logs[:1])
    return jnp.concatenate([zero_row, delta], 0) - jnp.concatenate([delta, zero_row], 0)


def reference(primary, conductivity, anchor_x, owner, gate_index, misfit):
    times = 0.1 * jnp.float32(15.0) ** (gate_index.astype(jnp.float32) / jnp.float32(NTIMES - 1))
    stacked = jnp.concatenate([primary[:, :FZ].astype(jnp.float32), conductivity[None, :FZ].astype(jnp.float32)], 0)
    grid = stacked.reshape(4, FZ, N_ROW, N_DEV, TY, TX).transpose(0, 1, 2, 4, 3, 5).reshape(4, FZ, GY, GX)
    padded = jnp.pad(grid, ((0, 0), (0, 0), (HALO, HALO), (0, 0)))
    blocks = jnp.repeat(jnp.arange(N_ROW, dtype=jnp.int32), FOOT_ROW)
    anchors = anchor_x.reshape(-1).astype(jnp.int32)
    residues = misfit.reshape(-1, GATES)

    def one(carry, item):
        block, anchor, res = item
        zero = jnp.zeros((), jnp.int32)
        window = lax.dynamic_slice(padded, (zero, zero, block * TY, anchor), (4, FZ, FP, FP))
        lam, local = footprint(window, res, times)
        current = lax.dynamic_slice(carry, (zero, block * TY, anchor), (FZ, FP, FP))
        carry = lax.dynamic_update_slice(carry, current + local, (zero, block * TY, anchor))
        return carry, lam

    start = jnp.zeros((FZ, GY + 2 * HALO, GX), jnp.float32)
    total, lams = lax.scan(one, start, (blocks, anchors, residues))
    data = total[:, HALO:HALO + GY]
    data = data.reshape(FZ, N_ROW, TY, N_DEV, TX).transpose(0, 1, 3, 2, 4).reshape(FZ, GCOLS)
    gradient = regularize(conductivity)
    gradient = gradient.at[:FZ].add(data)
    index = jnp.arange(FOOT_ROW, dtype=jnp.int32)
    same = owner[:, :, None] == owner[:, None, :]
    rank = jnp.sum((same & (index[None, None, :] < index[None, :, None])).astype(jnp.int32), axis=2)
    slot = ((jnp.arange(N_ROW, dtype=jnp.int32)[:, None] * N_DEV + owner) * MOST + rank).reshape(-1)
    adjoint_field = jnp.zeros((SLOTS, 3, FZ, FP * FP), jnp.float32)
    adjoint_field = adjoint_field.at[slot].set(lams.reshape(-1, 3, FZ, FP * FP))
    return gradient, adjoint_field
```

```python
import jax
import jax.numpy as jnp
from jax import lax
from jax.experimental import pallas as pl
from jax.experimental.pallas import tpu as pltpu
from jax.sharding import PartitionSpec as P

TX = 32
TY = 32
FZ = 40
FP = 48
GATES = 30
NTIMES = 64
STEPS = 2
MOST = 2
FOOT_ROW = 16
HALO = 8
N_DEV = 16
STEP = 0.05

LANES = FP * FP
QROWS = 12
QIN = QROWS * TX
BLOCK = MOST * QROWS * FP
BAND = FP * TX
LOG2E = 1.4426950408889634
LN15 = 2.70805020110221


def lane_iota(rows):
    return lax.broadcasted_iota(jnp.int32, (rows, 128), 1)


def cut_kernel(anchor, owner, tiles, out, count):
    for e in range(N_DEV):
        count[e] = 0
    lane = lane_iota(8)
    rows = []
    for v in range(5):
        at = lane + 128 * v
        y = sum((at >= FP * j).astype(jnp.int32) for j in range(1, QROWS + 1))
        rows.append((y, at - FP * y))

    def one(f, carry):
        o, e = anchor[0, f], owner[0, f]
        k = count[e]
        count[e] = k + 1
        d0, s = o // TX, o % TX
        full = pl.multiple_of(640 * k, 128)
        for v in range(5):
            y_of, x_of = rows[v]
            code = y_of * 4 + lax.shift_right_logical(x_of + s, 5)
            acc = jnp.zeros((FZ, 128), jnp.float32)
            for y in range(QROWS):
                if FP * y >= 128 * (v + 1) or FP * (y + 1) <= 128 * v:
                    continue
                for t in range(3):
                    src = tiles[jnp.minimum(d0 + t, N_DEV - 1), :, 128 * (y // 4) : 128 * (y // 4) + 128]
                    shift = (FP * y - TX * (y % 4) + TX * t - s) % 128
                    turned = pltpu.roll(src.astype(jnp.float32), shift, 1)
                    mask = code == 4 * y + t
                    acc = jnp.where(jnp.concatenate([mask] * 5, 0), turned, acc)
            if v < 4:
                out[e, :, pl.ds(full + 128 * v, 128)] = acc.astype(jnp.bfloat16)
            else:
                held = out[e, :, 512:640].astype(jnp.float32)
                low = lane_iota(FZ) < 64
                first = jnp.where(k == 0, acc, held)
                out[e, :, 512:640] = jnp.where(low, first, pltpu.roll(acc, 64, 1)).astype(jnp.bfloat16)
        return carry

    lax.fori_loop(0, FOOT_ROW, one, 0)


def solve_kernel(me_ref, anchor, owner, gates, misfit, parts, lam_out, canvas, window, lam, curl, local, x_masks):
    me = me_ref[0]
    cnt = jnp.int32(0)
    mine = [jnp.int32(0), jnp.int32(0)]
    for f in range(FOOT_ROW):
        hit = owner[0, f] == me
        for k in range(MOST):
            mine[k] = jnp.where(hit & (cnt == k), f, mine[k])
        cnt = cnt + hit.astype(jnp.int32)

    canvas[...] = jnp.zeros_like(canvas)
    lam[:, FZ:, :] = jnp.zeros((3, 8, LANES), jnp.float32)
    curl[:, :8, :] = jnp.zeros((3, 8, LANES), jnp.float32)
    x_of = lax.broadcasted_iota(jnp.int32, (8, LANES), 1) % FP
    x_masks[0] = (x_of != FP - 1).astype(jnp.float32)
    x_masks[1] = (x_of != 0).astype(jnp.float32)
    times = 0.1 * jnp.exp((LN15 / (NTIMES - 1)) * gates[...].astype(jnp.float32))
    scaled = -LOG2E * times
    all_lanes = lax.broadcasted_iota(jnp.int32, (8, LANES), 1)
    last_y = all_lanes >= LANES - FP
    first_y = all_lanes < FP

    def ahead_x(v):
        return pltpu.roll(v, LANES - 1, 1) * x_masks[0]

    def behind_x(v):
        return pltpu.roll(v, 1, 1) * x_masks[1]

    def ahead_y(v):
        return jnp.where(last_y, 0.0, pltpu.roll(v, LANES - FP, 1))

    def behind_y(v):
        return jnp.where(first_y, 0.0, pltpu.roll(v, FP, 1))

    for k in range(MOST):

        @pl.when(cnt <= k)
        def _(k=k):
            lam_out[k] = jnp.zeros((3, FZ, LANES), jnp.float32)

        @pl.when(cnt > k)
        def _(k=k):
            f = mine[k]
            o = anchor[0, f]
            low = lane_iota(FZ) < 64
            for c in range(4):
                for half in range(2):
                    base = 1152 * half
                    p, q = 4 * c + 2 * half, 4 * c + 2 * half + 1
                    full = slice(640 * k, 640 * k + 512)
                    pf = parts[p, :, full].astype(jnp.float32)
                    qf = pltpu.roll(parts[q, :, full].astype(jnp.float32), 64, 1)
                    ph = parts[p, :, 512:640].astype(jnp.float32)
                    qh = parts[q, :, 512:640].astype(jnp.float32)
                    if k == 0:
                        qh = pltpu.roll(qh, 64, 1)
                    else:
                        ph = pltpu.roll(ph, 64, 1)
                    window[c, :, base : base + 512] = pf
                    window[c, :, base + 512 : base + 640] = jnp.where(low, ph, qf[:, :128])
                    window[c, :, base + 640 : base + 1024] = qf[:, 128:]
                    window[c, :, base + 1024 : base + 1152] = jnp.where(low, qf[:, :128], qh)
            residue = misfit[pl.ds(f, 1), :]
            t_of = [jnp.broadcast_to(scaled[:, g : g + 1], (8, 128)) for g in range(GATES)]
            r_of = [jnp.broadcast_to(residue[:, g : g + 1], (8, 128)) for g in range(GATES)]

            def weigh(i, carry):
                z = pl.ds(pl.multiple_of(8 * i, 8), 8)
                for c0 in range(0, LANES, 384):
                    at = slice(c0, c0 + 384)
                    sigma = window[3, z, at]
                    weight = jnp.zeros_like(sigma)
                    for g in range(GATES):
                        t3 = jnp.concatenate([t_of[g]] * 3, 1)
                        r3 = jnp.concatenate([r_of[g]] * 3, 1)
                        weight = weight + r3 * jnp.exp2(sigma * t3)
                    for c in range(3):
                        lam[c, z, at] = weight * window[c, z, at]
                return carry

            lax.fori_loop(0, FZ // 8, weigh, 0)

            def step(n, carry):
                for i in range(FZ // 8):
                    z = slice(8 * i, 8 * i + 8)
                    up = slice(8 * i + 1, 8 * i + 9)
                    vx, vy, vz = lam[0, z, :], lam[1, z, :], lam[2, z, :]
                    at = slice(8 * i + 8, 8 * i + 16)
                    curl[0, at, :] = (ahead_y(vz) - vz) - (lam[1, up, :] - vy)
                    curl[1, at, :] = (lam[0, up, :] - vx) - (ahead_x(vz) - vz)
                    curl[2, at, :] = (ahead_x(vy) - vy) - (ahead_y(vx) - vx)
                for i in range(FZ // 8):
                    z = slice(8 * i, 8 * i + 8)
                    at = slice(8 * i + 8, 8 * i + 16)
                    down = slice(8 * i + 7, 8 * i + 15)
                    wx, wy, wz = curl[0, at, :], curl[1, at, :], curl[2, at, :]
                    ux = (curl[1, down, :] - wy) - (behind_y(wz) - wz)
                    uy = (behind_x(wz) - wz) - (curl[0, down, :] - wx)
                    uz = (behind_y(wx) - wx) - (behind_x(wy) - wy)
                    sigma = window[3, z, :]
                    for c, u in enumerate((ux, uy, uz)):
                        v = lam[c, z, :]
                        lam[c, z, :] = v - STEP * (u + sigma * v)
                return carry

            lax.fori_loop(0, STEPS, step, 0)
            for i in range(FZ // 8):
                z = slice(8 * i, 8 * i + 8)
                total = None
                for c in range(3):
                    v = lam[c, z, :]
                    lam_out[k, c, z, :] = v
                    term = v * window[c, z, :]
                    total = term if total is None else total + term
                local[z, :] = total
            d0, s = o // TX, o % TX
            lane = lane_iota(8)
            row_in, x_in = lane // TX, lane % TX

            def place(t, carry):
                d = jnp.minimum(d0 + t, N_DEV - 1)
                xw = x_in + (TX * t - s)
                inside = (xw >= 0) & (xw < FP)
                for v in range(FP // 4):
                    acc = canvas[d, :, 128 * v : 128 * v + 128]
                    for j in range(4):
                        y = 4 * v + j
                        a = FP * y // 128
                        spill = 128 * (a + 1) - FP * y
                        shift = (TX * j - FP * y + s - TX * t) % 128
                        for b in range(2 if spill < FP else 1):
                            mask = inside & (row_in == j)
                            if spill < FP:
                                mask = mask & ((xw >= spill) if b else (xw < spill))
                            src = local[:, 128 * (a + b) : 128 * (a + b) + 128]
                            turned = pltpu.roll(src, shift, 1)
                            acc = acc + jnp.where(jnp.concatenate([mask] * 5, 0), turned, 0.0)
                    canvas[d, :, 128 * v : 128 * v + 128] = acc
                return carry

            lax.fori_loop(0, 3, place, 0)


def regularize(conductivity):
    logs = jnp.log(conductivity.astype(jnp.float32))
    delta = logs[1:] - logs[:-1]
    zero_row = jnp.zeros_like(logs[:1])
    return jnp.concatenate([zero_row, delta], 0) - jnp.concatenate([delta, zero_row], 0)


def neighbours(first, last, axis):
    peers = lax.axis_size(axis)
    up = [(i, i + 1) for i in range(peers - 1)]
    down = [(i + 1, i) for i in range(peers - 1)]
    return lax.ppermute(last, axis, up), lax.ppermute(first, axis, down)


SMEM = pl.BlockSpec(memory_space=pltpu.SMEM)
VMEM = pl.BlockSpec(memory_space=pltpu.VMEM)
LIMIT = 48 * 2**20


def per_device(primary, conductivity, anchor_x, owner, gate_index, misfit):
    me = lax.axis_index("dev").astype(jnp.int32).reshape(1)
    tile = jnp.concatenate([primary[:, :FZ], conductivity[None, :FZ]], axis=0)
    halo = HALO * TX
    before, after = neighbours(tile[..., :halo], tile[..., -halo:], "row")
    chunks = [
        jnp.concatenate([before, tile[..., : QIN - halo]], -1),
        tile[..., QIN - halo : 2 * QIN - halo],
        tile[..., 2 * QIN - halo : 3 * QIN - halo],
        jnp.concatenate([tile[..., 3 * QIN - halo :], after], -1),
    ]
    spread = jnp.stack(chunks, 1).reshape(N_DEV, FZ, QIN)
    spread = lax.all_to_all(spread, "dev", 0, 0, tiled=True)
    windows = pl.pallas_call(
        cut_kernel,
        out_shape=jax.ShapeDtypeStruct((N_DEV, FZ, BLOCK), jnp.bfloat16),
        in_specs=[SMEM, SMEM, VMEM],
        out_specs=VMEM,
        scratch_shapes=[pltpu.SMEM((N_DEV,), jnp.int32)],
        compiler_params=pltpu.CompilerParams(vmem_limit_bytes=LIMIT),
        name="cut",
    )(anchor_x, owner, spread)
    parts = lax.all_to_all(windows, "dev", 0, 0, tiled=True)
    adjoint_field, canvas = pl.pallas_call(
        solve_kernel,
        out_shape=(
            jax.ShapeDtypeStruct((MOST, 3, FZ, LANES), jnp.float32),
            jax.ShapeDtypeStruct((N_DEV, FZ, BAND), jnp.float32),
        ),
        in_specs=[SMEM, SMEM, SMEM, VMEM, VMEM, VMEM],
        out_specs=(VMEM, VMEM),
        scratch_shapes=[
            pltpu.VMEM((4, FZ, LANES), jnp.float32),
            pltpu.VMEM((3, FZ + 8, LANES), jnp.float32),
            pltpu.VMEM((3, FZ + 8, LANES), jnp.float32),
            pltpu.VMEM((FZ, LANES), jnp.float32),
            pltpu.VMEM((2, 8, LANES), jnp.float32),
        ],
        compiler_params=pltpu.CompilerParams(vmem_limit_bytes=LIMIT),
        name="solve",
    )(me, anchor_x, owner, gate_index.reshape(1, GATES), misfit[0], parts)
    summed = jnp.sum(lax.all_to_all(canvas, "dev", 0, 0, tiled=True), axis=0)
    from_before, from_after = neighbours(summed[:, :halo], summed[:, -halo:], "row")
    data = summed[:, halo:-halo]
    data = data + jnp.pad(from_before, ((0, 0), (0, TX * TY - halo)))
    data = data + jnp.pad(from_after, ((0, 0), (TX * TY - halo, 0)))
    gradient = regularize(conductivity)
    gradient = gradient + jnp.pad(data, ((0, gradient.shape[0] - FZ), (0, 0)))
    return gradient, adjoint_field


def solution(mesh):
    in_specs = (
        P(None, None, ("row", "dev")),
        P(None, ("row", "dev")),
        P("row", None),
        P("row", None),
        P(),
        P("row", None, None),
    )
    out_specs = (P(None, ("row", "dev")), P(("row", "dev"), None, None, None))
    return jax.shard_map(
        per_device, mesh=mesh, in_specs=in_specs, out_specs=out_specs, check_vma=False
    )
```

```python
import jax
import jax.numpy as jnp
from jax import lax
from jax.experimental import pallas as pl
from jax.experimental.pallas import tpu as pltpu
from jax.sharding import PartitionSpec as P

TX = 32
TY = 32
FZ = 40
FP = 48
GATES = 30
NTIMES = 64
STEPS = 2
MOST = 2
FOOT_ROW = 16
HALO = 8
N_DEV = 16
STEP = 0.05

LANES = FP * FP
QROWS = 12
QIN = QROWS * TX
CUT = 640
RROWS = 3
BACK = 896
UNROLL = 4
LOG2E = 1.4426950408889634
LN15 = 2.70805020110221


def turn(v, by):
    return pltpu.roll(v, by % 128, 1)


def lane_iota(rows):
    return lax.broadcasted_iota(jnp.int32, (rows, 128), 1)


def tall(mask):
    return jnp.concatenate([mask] * (FZ // 8), 0)


def assign(owner, table, seconds):
    for e in range(N_DEV):
        table[0, e] = -1
        table[1, e] = -1
    for f in range(FOOT_ROW):
        e = owner[0, f]
        held, other = table[0, e], table[1, e]
        table[0, e] = jnp.where(held >= 0, held, f)
        table[1, e] = jnp.where(held >= 0, f, other)
    n = jnp.int32(0)
    for e in range(N_DEV):
        other = table[1, e]
        seconds[n] = other
        n = n + (other >= 0).astype(jnp.int32)
    n = jnp.int32(0)
    for e in range(N_DEV):
        held = table[0, e]
        table[2, e] = (held >= 0).astype(jnp.int32)
        table[0, e] = jnp.where(held >= 0, held, seconds[n])
        n = n + (held < 0).astype(jnp.int32)


def cut_kernel(anchor, owner, tiles, out, second, table, seconds):
    assign(owner, table, seconds)
    row_in = lane_iota(8) // TX
    picks = []
    for v in range(5):
        at = lane_iota(8) + 128 * v
        y = sum((at >= FP * j).astype(jnp.int32) for j in range(1, QROWS + 1))
        picks.append((y, at - FP * y))

    def one(e, carry):
        f = table[0, e]
        o, w = anchor[0, f], owner[0, f]
        d0, s = o // TX, o % TX
        made = [jnp.zeros((FZ, 128), jnp.float32) for _ in range(5)]
        codes = [8 * (y // 4) + y % 4 + 2 * lax.shift_right_logical(x + s, 5) for y, x in picks]
        for m in range(QROWS // 4):
            tile = [
                tiles[jnp.minimum(d0 + t, N_DEV - 1), :, 128 * m : 128 * m + 128].astype(jnp.float32) for t in range(3)
            ]
            for n in range(8):
                from_t = [t for t in range(3) if 0 <= n - 2 * t < 4]
                src = tile[from_t[0]]
                for t in from_t[1:]:
                    src = jnp.where(tall(row_in == n - 2 * t), tile[t], src)
                turned = turn(src, 192 * m + 16 * n - s)
                rows = [(n - 2 * t, t) for t in from_t]
                for v in range(5):
                    if any(
                        192 * m + FP * j + max(0, TX * t - 31) < 128 * (v + 1)
                        and 192 * m + FP * j + min(FP, TX * (t + 1)) > 128 * v
                        for j, t in rows
                    ):
                        made[v] = jnp.where(tall(codes[v] == 8 * m + n), turned, made[v])
        for v in range(5):
            out[e, :, 128 * v : 128 * v + 128] = made[v].astype(jnp.bfloat16)

        @pl.when(table[1, w] == f)
        def _():
            second[w] = out[e]

        return carry

    lax.fori_loop(0, N_DEV, one, 0)


def adjoint(f, gates, misfit, parts, window, lam, curl, x_masks):
    lam[:, FZ:, :] = jnp.zeros((3, 8, LANES), jnp.float32)
    curl[:, :8, :] = jnp.zeros((3, 8, LANES), jnp.float32)
    x_of = lax.broadcasted_iota(jnp.int32, (8, LANES), 1) % FP
    x_masks[0] = (x_of != FP - 1).astype(jnp.float32)
    x_masks[1] = (x_of != 0).astype(jnp.float32)
    times = 0.1 * jnp.exp((LN15 / (NTIMES - 1)) * gates[...].astype(jnp.float32))
    scaled = -LOG2E * times
    all_lanes = lax.broadcasted_iota(jnp.int32, (8, LANES), 1)
    last_y = all_lanes >= LANES - FP
    first_y = all_lanes < FP

    def ahead_x(v):
        return pltpu.roll(v, LANES - 1, 1) * x_masks[0]

    def behind_x(v):
        return pltpu.roll(v, 1, 1) * x_masks[1]

    def ahead_y(v):
        return jnp.where(last_y, 0.0, pltpu.roll(v, LANES - FP, 1))

    def behind_y(v):
        return jnp.where(first_y, 0.0, pltpu.roll(v, FP, 1))

    low = lane_iota(FZ) < 64
    for c in range(4):
        for half in range(2):
            base = 1152 * half
            p, q = 4 * c + 2 * half, 4 * c + 2 * half + 1
            pf = parts[p, :, :512].astype(jnp.float32)
            qf = pltpu.roll(parts[q, :, :512].astype(jnp.float32), 64, 1)
            ph = parts[p, :, 512:640].astype(jnp.float32)
            qh = turn(parts[q, :, 512:640].astype(jnp.float32), 64)
            window[c, :, base : base + 512] = pf
            window[c, :, base + 512 : base + 640] = jnp.where(low, ph, qf[:, :128])
            window[c, :, base + 640 : base + 1024] = qf[:, 128:]
            window[c, :, base + 1024 : base + 1152] = jnp.where(low, qf[:, :128], qh)
    residue = misfit[pl.ds(f, 1), :]
    t_of = [jnp.broadcast_to(scaled[:, g : g + 1], (8, 128)) for g in range(GATES)]
    r_of = [jnp.broadcast_to(residue[:, g : g + 1], (8, 128)) for g in range(GATES)]

    def weigh(i, carry):
        z = pl.ds(pl.multiple_of(8 * i, 8), 8)
        for c0 in range(0, LANES, 384):
            at = slice(c0, c0 + 384)
            sigma = window[3, z, at]
            weight = jnp.zeros_like(sigma)
            for g in range(GATES):
                t3 = jnp.concatenate([t_of[g]] * 3, 1)
                r3 = jnp.concatenate([r_of[g]] * 3, 1)
                weight = weight + r3 * jnp.exp2(sigma * t3)
            for c in range(3):
                lam[c, z, at] = weight * window[c, z, at]
        return carry

    lax.fori_loop(0, FZ // 8, weigh, 0)

    def step(n, carry):
        for i in range(FZ // 8):
            z = slice(8 * i, 8 * i + 8)
            up = slice(8 * i + 1, 8 * i + 9)
            vx, vy, vz = lam[0, z, :], lam[1, z, :], lam[2, z, :]
            at = slice(8 * i + 8, 8 * i + 16)
            curl[0, at, :] = (ahead_y(vz) - vz) - (lam[1, up, :] - vy)
            curl[1, at, :] = (lam[0, up, :] - vx) - (ahead_x(vz) - vz)
            curl[2, at, :] = (ahead_x(vy) - vy) - (ahead_y(vx) - vx)
        for i in range(FZ // 8):
            z = slice(8 * i, 8 * i + 8)
            at = slice(8 * i + 8, 8 * i + 16)
            down = slice(8 * i + 7, 8 * i + 15)
            wx, wy, wz = curl[0, at, :], curl[1, at, :], curl[2, at, :]
            ux = (curl[1, down, :] - wy) - (behind_y(wz) - wz)
            uy = (behind_x(wz) - wz) - (curl[0, down, :] - wx)
            uz = (behind_y(wx) - wx) - (behind_x(wy) - wy)
            sigma = window[3, z, :]
            for c, u in enumerate((ux, uy, uz)):
                v = lam[c, z, :]
                lam[c, z, :] = v - STEP * (u + sigma * v)
        return carry

    lax.fori_loop(0, STEPS, step, 0)


def solve_kernel(me, table, gates, misfit, parts, second, adjoint_out, back, window, lam, curl, local, x_masks, sem):
    f, own = table[0, me[0]], table[2, me[0]]
    adjoint(f, gates, misfit, parts, window, lam, curl, x_masks)
    for i in range(FZ // 8):
        z = slice(8 * i, 8 * i + 8)
        total = None
        for c in range(3):
            v = lam[c, z, :]
            lam[c, z, :] = jnp.where(own == 1, v, 0.0)
            term = v * window[c, z, :]
            total = term if total is None else total + term
        local[z, :] = total
    copy = pltpu.make_async_copy(lam.at[:, :FZ, :], adjoint_out.at[0], sem)
    copy.start()
    lane = lane_iota(FZ)
    for j in range(N_DEV):
        a, r = 144 * j // 128, 144 * j % 128
        both = [local[:, 128 * (a + b) : 128 * (a + b) + 128] for b in range(2)]
        high = [v.astype(jnp.bfloat16).astype(jnp.float32) for v in both]
        rest = [turn(v - h, 80 - r) for v, h in zip(both, high)]
        high = [turn(h, 64 - r) for h in high]
        back[j, :, :512] = second[j, :, :512]
        v4 = jnp.where(lane - 64 < 128 - r, high[0], high[1])
        v4 = jnp.where(lane < 64, second[j, :, 512:640].astype(jnp.float32), v4)
        v5 = jnp.where(lane + 64 < 128 - r, high[0], high[1])
        v5 = jnp.where(lane < 80, v5, jnp.where(lane - 80 < 128 - r, rest[0], rest[1]))
        v6 = jnp.where(lane + 48 < 128 - r, rest[0], rest[1])
        for b, v in enumerate((v4, v5, v6)):
            back[j, :, 512 + 128 * b : 640 + 128 * b] = v.astype(jnp.bfloat16)
    copy.wait()


def second_kernel(me, table, gates, misfit, parts, adjoint_in, adjoint_out, window, lam, curl, x_masks, sem):
    del adjoint_in
    f = table[1, me[0]]

    @pl.when(f >= 0)
    def _():
        adjoint(f, gates, misfit, parts, window, lam, curl, x_masks)

    @pl.when(f < 0)
    def _():
        lam[:, :FZ, :] = jnp.zeros((3, FZ, LANES), jnp.float32)

    copy = pltpu.make_async_copy(lam.at[:, :FZ, :], adjoint_out.at[1], sem)
    copy.start()
    copy.wait()


def scatter_kernel(anchor, table, back, out):
    out[...] = jnp.zeros_like(out)
    lane = lane_iota(FZ)
    row_in, x_in = lane_iota(8) // TX, lane_iota(8) % TX

    def one(e, carry):
        o = anchor[0, table[0, e]]
        d0, s = o // TX, o % TX
        v4, v5, v6 = (back[e, :, 512 + 128 * b : 640 + 128 * b].astype(jnp.float32) for b in range(3))
        r5, s6 = turn(v5, 64), turn(v6, 48)
        first = jnp.where(lane < 64, turn(v4, 64), r5) + jnp.where(lane < 48, turn(v5, 48), s6)
        rest = r5 + s6
        moved = [turn(first, s - 16 * n) for n in range(6)] + [turn(jnp.where(lane < 16, rest, first), s - 96)]
        spilt = {2: turn(rest, s - 32), 4: turn(rest, s - 64), 6: moved[6]}
        for t in range(3):
            xw = x_in + (TX * t - s)
            inside = (xw >= 0) & (xw < FP)
            add = jnp.where(tall(inside & (row_in == 0)), moved[2 * t], 0.0)
            add = jnp.where(tall(inside & (row_in == 1)), moved[2 * t + 1], add)
            add = jnp.where(tall(inside & (row_in == 2) & (xw < 32)), moved[2 * t + 2], add)
            add = jnp.where(tall(inside & (row_in == 2) & (xw >= 32)), spilt[2 * t + 2], add)
            d = jnp.minimum(d0 + t, N_DEV - 1)
            out[d] = out[d] + add
        return carry

    lax.fori_loop(0, N_DEV, one, 0, unroll=UNROLL)


def join_kernel(sums, first, own, last):
    lane = lane_iota(FZ)
    made = []
    for g in range(0, N_DEV, 4):
        a = sums[g]
        b, c, d = (turn(sums[g + n], 128 - 32 * n) for n in range(1, 4))
        made += [jnp.where(lane < 96, a, b), jnp.where(lane < 64, b, c), jnp.where(lane < 32, c, d)]
    for n in range(2):
        first[:, 128 * n : 128 * n + 128] = made[n]
        last[:, 128 * n : 128 * n + 128] = made[10 + n]
    for n in range(8):
        own[:, 128 * n : 128 * n + 128] = made[2 + n]


def regularize(conductivity):
    logs = jnp.log(conductivity.astype(jnp.float32))
    delta = logs[1:] - logs[:-1]
    zero_row = jnp.zeros_like(logs[:1])
    return jnp.concatenate([zero_row, delta], 0) - jnp.concatenate([delta, zero_row], 0)


def neighbours(first, last, axis):
    peers = lax.axis_size(axis)
    up = [(i, i + 1) for i in range(peers - 1)]
    down = [(i + 1, i) for i in range(peers - 1)]
    return lax.ppermute(last, axis, up), lax.ppermute(first, axis, down)


SMEM = pl.BlockSpec(memory_space=pltpu.SMEM)
VMEM = pl.BlockSpec(memory_space=pltpu.VMEM)
ANY = pl.BlockSpec(memory_space=pl.ANY)
PARAMS = pltpu.CompilerParams(vmem_limit_bytes=40 * 2**20)
F32 = jnp.float32
WORK = [
    pltpu.VMEM((4, FZ, LANES), F32),
    pltpu.VMEM((3, FZ + 8, LANES), F32),
    pltpu.VMEM((3, FZ + 8, LANES), F32),
]
MASKS = pltpu.VMEM((2, 8, LANES), F32)


def exchange(blocks):
    return lax.all_to_all(blocks, "dev", 0, 0, tiled=True)


def per_device(primary, conductivity, anchor_x, owner, gate_index, misfit):
    me = lax.axis_index("dev").astype(jnp.int32).reshape(1)
    gates, residues = gate_index.reshape(1, GATES), misfit[0]
    tile = jnp.concatenate([primary[:, :FZ], conductivity[None, :FZ]], axis=0)
    halo = HALO * TX
    before, after = neighbours(tile[..., :halo], tile[..., -halo:], "row")
    chunks = [
        jnp.concatenate([before, tile[..., : QIN - halo]], -1),
        tile[..., QIN - halo : 2 * QIN - halo],
        tile[..., 2 * QIN - halo : 3 * QIN - halo],
        jnp.concatenate([tile[..., 3 * QIN - halo :], after], -1),
    ]
    spread = exchange(jnp.stack(chunks, 1).reshape(N_DEV, FZ, QIN))
    cut_shape = jax.ShapeDtypeStruct((N_DEV, FZ, CUT), jnp.bfloat16)
    windows, second, table = pl.pallas_call(
        cut_kernel,
        out_shape=(cut_shape, cut_shape, jax.ShapeDtypeStruct((3, N_DEV), jnp.int32)),
        in_specs=[SMEM, SMEM, VMEM],
        out_specs=(VMEM, VMEM, SMEM),
        scratch_shapes=[pltpu.SMEM((N_DEV + 1,), jnp.int32)],
        compiler_params=PARAMS,
        name="cut",
    )(anchor_x, owner, spread)
    adjoint_shape = jax.ShapeDtypeStruct((MOST, 3, FZ, LANES), F32)
    field, back = pl.pallas_call(
        solve_kernel,
        out_shape=(adjoint_shape, jax.ShapeDtypeStruct((N_DEV, FZ, BACK), jnp.bfloat16)),
        in_specs=[SMEM, SMEM, VMEM, VMEM, VMEM, VMEM],
        out_specs=(ANY, VMEM),
        scratch_shapes=[*WORK, pltpu.VMEM((FZ, LANES), F32), MASKS, pltpu.SemaphoreType.DMA],
        compiler_params=PARAMS,
        name="solve",
    )(me, table, gates, residues, exchange(windows), second)
    back = exchange(back)
    columns = pl.pallas_call(
        scatter_kernel,
        out_shape=jax.ShapeDtypeStruct((N_DEV, FZ, 128), F32),
        in_specs=[SMEM, SMEM, VMEM],
        out_specs=VMEM,
        compiler_params=PARAMS,
        name="scatter",
    )(anchor_x, table, back)
    adjoint_field = pl.pallas_call(
        second_kernel,
        out_shape=adjoint_shape,
        in_specs=[SMEM, SMEM, VMEM, VMEM, VMEM, ANY],
        out_specs=ANY,
        scratch_shapes=[*WORK, MASKS, pltpu.SemaphoreType.DMA],
        input_output_aliases={5: 0},
        compiler_params=PARAMS,
        cost_estimate=pl.CostEstimate(flops=2 * 10**7, bytes_accessed=4 * 10**6, transcendentals=3 * 10**6),
        name="second",
    )(me, table, gates, residues, back, field)
    sums, adjoint_field = lax.optimization_barrier((exchange(columns), adjoint_field))
    half = jax.ShapeDtypeStruct((FZ, halo), F32)
    first, own, last = pl.pallas_call(
        join_kernel,
        out_shape=(half, jax.ShapeDtypeStruct((FZ, TX * TY), F32), half),
        in_specs=[VMEM],
        out_specs=(VMEM, VMEM, VMEM),
        compiler_params=PARAMS,
        name="join",
    )(sums)
    from_before, from_after = neighbours(first, last, "row")
    data = own + jnp.pad(from_before, ((0, 0), (0, TX * TY - halo)))
    data = data + jnp.pad(from_after, ((0, 0), (TX * TY - halo, 0)))
    gradient = regularize(conductivity)
    gradient = gradient + jnp.pad(data, ((0, gradient.shape[0] - FZ), (0, 0)))
    return gradient, adjoint_field


def solution(mesh):
    in_specs = (
        P(None, None, ("row", "dev")),
        P(None, ("row", "dev")),
        P("row", None),
        P("row", None),
        P(),
        P("row", None, None),
    )
    out_specs = (P(None, ("row", "dev")), P(("row", "dev"), None, None, None))
    return jax.shard_map(
        per_device, mesh=mesh, in_specs=in_specs, out_specs=out_specs, check_vma=False
    )
```

```python
import jax
import jax.numpy as jnp
from jax import lax
from jax.experimental import pallas as pl
from jax.experimental.pallas import tpu as pltpu
from jax.sharding import PartitionSpec as P

TX = 32
TY = 32
FZ = 40
FP = 48
GATES = 30
NTIMES = 64
STEPS = 2
MOST = 2
FOOT_ROW = 16
HALO = 8
N_DEV = 16
STEP = 0.05

LANES = FP * FP
QROWS = 12
QIN = QROWS * TX
CUT = 640
RROWS = 3
BACK = 896
DEPTH = 48
UNROLL = 2
LOG2E = 1.4426950408889634
LN15 = 2.70805020110221


def turn(v, by):
    return pltpu.roll(v, by % 128, 1)


def lane_iota(rows):
    return lax.broadcasted_iota(jnp.int32, (rows, 128), 1)


def tall(mask):
    return jnp.concatenate([mask] * (FZ // 8), 0)


def assign_kernel(owner, table, seconds):
    for e in range(N_DEV):
        table[0, e] = -1
        table[1, e] = -1
    for f in range(FOOT_ROW):
        e = owner[0, f]
        held, other = table[0, e], table[1, e]
        table[0, e] = jnp.where(held >= 0, held, f)
        table[1, e] = jnp.where(held >= 0, f, other)
    n = jnp.int32(0)
    for e in range(N_DEV):
        other = table[1, e]
        seconds[n] = other
        n = n + (other >= 0).astype(jnp.int32)
    n = jnp.int32(0)
    for e in range(N_DEV):
        held = table[0, e]
        table[2, e] = (held >= 0).astype(jnp.int32)
        table[0, e] = jnp.where(held >= 0, held, seconds[n])
        n = n + (held < 0).astype(jnp.int32)


def edge_kernel(primary, conductivity, first, last, held, sems):
    width = first.shape[-1]
    copies = []
    for n, start in enumerate((0, conductivity.shape[-1] - width)):
        at = slice(start, start + width)
        copies.append(pltpu.make_async_copy(primary.at[:, :DEPTH, at], held.at[n, :3], sems.at[2 * n]))
        copies.append(pltpu.make_async_copy(conductivity.at[:DEPTH, at], held.at[n, 3], sems.at[2 * n + 1]))
    for copy in copies:
        copy.start()
    for copy in copies:
        copy.wait()
    first[...] = held[0, :, :FZ, :]
    last[...] = held[1, :, :FZ, :]


def tile_kernel(primary, conductivity, out, held, sems):
    copies = [
        pltpu.make_async_copy(primary.at[:, :DEPTH], held.at[:3], sems.at[0]),
        pltpu.make_async_copy(conductivity.at[:DEPTH], held.at[3], sems.at[1]),
    ]
    for copy in copies:
        copy.start()
    for copy in copies:
        copy.wait()
    out[...] = held[:, :FZ, :]


def cut_kernel(anchor, owner, table, tiles, out, second):
    row_in = lane_iota(8) // TX
    picks = []
    for v in range(5):
        at = lane_iota(8) + 128 * v
        y = sum((at >= FP * j).astype(jnp.int32) for j in range(1, QROWS + 1))
        picks.append((y, at - FP * y))

    def one(e, carry):
        f = table[0, e]
        o, w = anchor[0, f], owner[0, f]
        d0, s = o // TX, o % TX
        made = [jnp.zeros((FZ, 128), jnp.float32) for _ in range(5)]
        codes = [8 * (y // 4) + y % 4 + 2 * lax.shift_right_logical(x + s, 5) for y, x in picks]
        for m in range(QROWS // 4):
            tile = [
                tiles[jnp.minimum(d0 + t, N_DEV - 1), :, 128 * m : 128 * m + 128].astype(jnp.float32) for t in range(3)
            ]
            for n in range(8):
                from_t = [t for t in range(3) if 0 <= n - 2 * t < 4]
                src = tile[from_t[0]]
                for t in from_t[1:]:
                    src = jnp.where(tall(row_in == n - 2 * t), tile[t], src)
                turned = turn(src, 192 * m + 16 * n - s)
                rows = [(n - 2 * t, t) for t in from_t]
                for v in range(5):
                    if any(
                        192 * m + FP * j + max(0, TX * t - 31) < 128 * (v + 1)
                        and 192 * m + FP * j + min(FP, TX * (t + 1)) > 128 * v
                        for j, t in rows
                    ):
                        made[v] = jnp.where(tall(codes[v] == 8 * m + n), turned, made[v])
        for v in range(5):
            out[e, :, 128 * v : 128 * v + 128] = made[v].astype(jnp.bfloat16)

        @pl.when(table[1, w] == f)
        def _():
            second[w] = out[e]

        return carry

    lax.fori_loop(0, N_DEV, one, 0)


def adjoint(f, gates, misfit, parts, window, lam, curl, x_masks):
    lam[:, FZ:, :] = jnp.zeros((3, 8, LANES), jnp.float32)
    curl[:, :8, :] = jnp.zeros((3, 8, LANES), jnp.float32)
    x_of = lax.broadcasted_iota(jnp.int32, (8, LANES), 1) % FP
    x_masks[0] = (x_of != FP - 1).astype(jnp.float32)
    x_masks[1] = (x_of != 0).astype(jnp.float32)
    times = 0.1 * jnp.exp((LN15 / (NTIMES - 1)) * gates[...].astype(jnp.float32))
    scaled = -LOG2E * times
    all_lanes = lax.broadcasted_iota(jnp.int32, (8, LANES), 1)
    last_y = all_lanes >= LANES - FP
    first_y = all_lanes < FP

    def ahead_x(v):
        return pltpu.roll(v, LANES - 1, 1) * x_masks[0]

    def behind_x(v):
        return pltpu.roll(v, 1, 1) * x_masks[1]

    def ahead_y(v):
        return jnp.where(last_y, 0.0, pltpu.roll(v, LANES - FP, 1))

    def behind_y(v):
        return jnp.where(first_y, 0.0, pltpu.roll(v, FP, 1))

    low = lane_iota(FZ) < 64
    for c in range(4):
        for half in range(2):
            base = 1152 * half
            p, q = 4 * c + 2 * half, 4 * c + 2 * half + 1
            pf = parts[p, :, :512].astype(jnp.float32)
            qf = pltpu.roll(parts[q, :, :512].astype(jnp.float32), 64, 1)
            ph = parts[p, :, 512:640].astype(jnp.float32)
            qh = turn(parts[q, :, 512:640].astype(jnp.float32), 64)
            window[c, :, base : base + 512] = pf
            window[c, :, base + 512 : base + 640] = jnp.where(low, ph, qf[:, :128])
            window[c, :, base + 640 : base + 1024] = qf[:, 128:]
            window[c, :, base + 1024 : base + 1152] = jnp.where(low, qf[:, :128], qh)
    residue = misfit[pl.ds(f, 1), :]
    t_of = [jnp.broadcast_to(scaled[:, g : g + 1], (8, 128)) for g in range(GATES)]
    r_of = [jnp.broadcast_to(residue[:, g : g + 1], (8, 128)) for g in range(GATES)]

    def weigh(i, carry):
        z = pl.ds(pl.multiple_of(8 * i, 8), 8)
        for c0 in range(0, LANES, 384):
            at = slice(c0, c0 + 384)
            sigma = window[3, z, at]
            weight = jnp.zeros_like(sigma)
            for g in range(GATES):
                t3 = jnp.concatenate([t_of[g]] * 3, 1)
                r3 = jnp.concatenate([r_of[g]] * 3, 1)
                weight = weight + r3 * jnp.exp2(sigma * t3)
            for c in range(3):
                lam[c, z, at] = weight * window[c, z, at]
        return carry

    lax.fori_loop(0, FZ // 8, weigh, 0)

    def step(n, carry):
        for i in range(FZ // 8):
            z = slice(8 * i, 8 * i + 8)
            up = slice(8 * i + 1, 8 * i + 9)
            vx, vy, vz = lam[0, z, :], lam[1, z, :], lam[2, z, :]
            at = slice(8 * i + 8, 8 * i + 16)
            curl[0, at, :] = (ahead_y(vz) - vz) - (lam[1, up, :] - vy)
            curl[1, at, :] = (lam[0, up, :] - vx) - (ahead_x(vz) - vz)
            curl[2, at, :] = (ahead_x(vy) - vy) - (ahead_y(vx) - vx)
        for i in range(FZ // 8):
            z = slice(8 * i, 8 * i + 8)
            at = slice(8 * i + 8, 8 * i + 16)
            down = slice(8 * i + 7, 8 * i + 15)
            wx, wy, wz = curl[0, at, :], curl[1, at, :], curl[2, at, :]
            ux = (curl[1, down, :] - wy) - (behind_y(wz) - wz)
            uy = (behind_x(wz) - wz) - (curl[0, down, :] - wx)
            uz = (behind_y(wx) - wx) - (behind_x(wy) - wy)
            sigma = window[3, z, :]
            for c, u in enumerate((ux, uy, uz)):
                v = lam[c, z, :]
                lam[c, z, :] = v - STEP * (u + sigma * v)
        return carry

    lax.fori_loop(0, STEPS, step, 0)


def solve_kernel(me, table, gates, misfit, parts, second, lam_out, back_to, window, lam, curl, local, back, x_masks, sems):
    windows = pltpu.make_async_copy(second.at[:, :, :512], back_to.at[:, :, :512], sems.at[0])
    windows.start()
    f, own = table[0, me[0]], table[2, me[0]]
    adjoint(f, gates, misfit, parts, window, lam, curl, x_masks)
    for i in range(FZ // 8):
        z = slice(8 * i, 8 * i + 8)
        total = None
        for c in range(3):
            v = lam[c, z, :]
            lam_out[c, z, :] = jnp.where(own == 1, v, 0.0)
            term = v * window[c, z, :]
            total = term if total is None else total + term
        local[z, :] = total
    lane = lane_iota(FZ)
    copies = [windows]
    for j in range(N_DEV):
        a, r = 144 * j // 128, 144 * j % 128
        both = [local[:, 128 * (a + b) : 128 * (a + b) + 128] for b in range(2)]
        high = [v.astype(jnp.bfloat16).astype(jnp.float32) for v in both]
        rest = [turn(v - h, 80 - r) for v, h in zip(both, high)]
        high = [turn(h, 64 - r) for h in high]
        v4 = jnp.where(lane - 64 < 128 - r, high[0], high[1])
        v4 = jnp.where(lane < 64, second[j, :, 512:640].astype(jnp.float32), v4)
        v5 = jnp.where(lane + 64 < 128 - r, high[0], high[1])
        v5 = jnp.where(lane < 80, v5, jnp.where(lane - 80 < 128 - r, rest[0], rest[1]))
        v6 = jnp.where(lane + 48 < 128 - r, rest[0], rest[1])
        for b, v in enumerate((v4, v5, v6)):
            back[j, :, 128 * b : 128 * b + 128] = v.astype(jnp.bfloat16)
        if j % 4 == 3:
            some = slice(j - 3, j + 1)
            copies.append(pltpu.make_async_copy(back.at[some], back_to.at[some, :, 512:], sems.at[1 + j // 4]))
            copies[-1].start()
    for copy in copies:
        copy.wait()


def second_kernel(me, table, gates, misfit, parts, own, adjoint_out, window, lam, curl, x_masks, sems):
    first = pltpu.make_async_copy(own, adjoint_out.at[0], sems.at[0])
    first.start()
    f = table[1, me[0]]

    @pl.when(f >= 0)
    def _():
        adjoint(f, gates, misfit, parts, window, lam, curl, x_masks)

    @pl.when(f < 0)
    def _():
        lam[:, :FZ, :] = jnp.zeros((3, FZ, LANES), jnp.float32)

    copy = pltpu.make_async_copy(lam.at[:, :FZ, :], adjoint_out.at[1], sems.at[1])
    copy.start()
    copy.wait()
    first.wait()


def regularize_kernel(conductivity, out):
    logs = jnp.log(conductivity[...].astype(jnp.float32))
    delta = logs[1:] - logs[:-1]
    zero_row = jnp.zeros_like(logs[:1])
    out[...] = jnp.concatenate([zero_row, delta], 0) - jnp.concatenate([delta, zero_row], 0)


def scatter_kernel(anchor, table, back, out):
    out[...] = jnp.zeros_like(out)
    lane = lane_iota(FZ)
    row_in, x_in = lane_iota(8) // TX, lane_iota(8) % TX

    def one(e, carry):
        o = anchor[0, table[0, e]]
        d0, s = o // TX, o % TX
        v4, v5, v6 = (back[e, :, 512 + 128 * b : 640 + 128 * b].astype(jnp.float32) for b in range(3))
        r5, s6 = turn(v5, 64), turn(v6, 48)
        first = jnp.where(lane < 64, turn(v4, 64), r5) + jnp.where(lane < 48, turn(v5, 48), s6)
        rest = r5 + s6
        moved = [turn(first, s - 16 * n) for n in range(6)] + [turn(jnp.where(lane < 16, rest, first), s - 96)]
        spilt = {2: turn(rest, s - 32), 4: turn(rest, s - 64), 6: moved[6]}
        for t in range(3):
            xw = x_in + (TX * t - s)
            inside = (xw >= 0) & (xw < FP)
            add = jnp.where(tall(inside & (row_in == 0)), moved[2 * t], 0.0)
            add = jnp.where(tall(inside & (row_in == 1)), moved[2 * t + 1], add)
            add = jnp.where(tall(inside & (row_in == 2) & (xw < 32)), moved[2 * t + 2], add)
            add = jnp.where(tall(inside & (row_in == 2) & (xw >= 32)), spilt[2 * t + 2], add)
            d = jnp.minimum(d0 + t, N_DEV - 1)
            out[d] = out[d] + add
        return carry

    lax.fori_loop(0, N_DEV, one, 0, unroll=UNROLL)


def join_kernel(sums, first, own, last):
    lane = lane_iota(FZ)
    made = []
    for g in range(0, N_DEV, 4):
        a = sums[g]
        b, c, d = (turn(sums[g + n], 128 - 32 * n) for n in range(1, 4))
        made += [jnp.where(lane < 96, a, b), jnp.where(lane < 64, b, c), jnp.where(lane < 32, c, d)]
    for n in range(2):
        first[:, 128 * n : 128 * n + 128] = made[n]
        last[:, 128 * n : 128 * n + 128] = made[10 + n]
    for n in range(8):
        own[:, 128 * n : 128 * n + 128] = made[2 + n]


def neighbours(first, last, axis):
    peers = lax.axis_size(axis)
    up = [(i, i + 1) for i in range(peers - 1)]
    down = [(i + 1, i) for i in range(peers - 1)]
    return lax.ppermute(last, axis, up), lax.ppermute(first, axis, down)


SMEM = pl.BlockSpec(memory_space=pltpu.SMEM)
VMEM = pl.BlockSpec(memory_space=pltpu.VMEM)
ANY = pl.BlockSpec(memory_space=pl.ANY)
PARAMS = pltpu.CompilerParams(vmem_limit_bytes=24 * 2**20)
F32 = jnp.float32
WIDE = 60 * 2**20
SMALL = pl.CostEstimate(flops=10**6, bytes_accessed=10**6, transcendentals=10**5)
WORK = [
    pltpu.VMEM((4, FZ, LANES), F32),
    pltpu.VMEM((3, FZ + 8, LANES), F32),
    pltpu.VMEM((3, FZ + 8, LANES), F32),
]
MASKS = pltpu.VMEM((2, 8, LANES), F32)


def exchange(blocks):
    return lax.all_to_all(blocks, "dev", 0, 0, tiled=True)


def per_device(primary, conductivity, anchor_x, owner, gate_index, misfit):
    me = lax.axis_index("dev").astype(jnp.int32).reshape(1)
    gates, residues = gate_index.reshape(1, GATES), misfit[0]
    halo = HALO * TX
    half = jax.ShapeDtypeStruct((4, FZ, halo), jnp.bfloat16)
    first, last = pl.pallas_call(
        edge_kernel,
        out_shape=(half, half),
        in_specs=[ANY, ANY],
        out_specs=(VMEM, VMEM),
        scratch_shapes=[pltpu.VMEM((2, 4, DEPTH, halo), jnp.bfloat16), pltpu.SemaphoreType.DMA((4,))],
        compiler_params=pltpu.CompilerParams(vmem_limit_bytes=WIDE),
        name="edges",
    )(primary, conductivity)
    before, after = neighbours(first, last, "row")
    tile = pl.pallas_call(
        tile_kernel,
        out_shape=jax.ShapeDtypeStruct((4, FZ, TX * TY), jnp.bfloat16),
        in_specs=[ANY, ANY],
        out_specs=VMEM,
        scratch_shapes=[pltpu.VMEM((4, DEPTH, TX * TY), jnp.bfloat16), pltpu.SemaphoreType.DMA((2,))],
        compiler_params=PARAMS,
        cost_estimate=SMALL,
        name="tile",
    )(primary, conductivity)
    chunks = [
        jnp.concatenate([before, tile[..., : QIN - halo]], -1),
        tile[..., QIN - halo : 2 * QIN - halo],
        tile[..., 2 * QIN - halo : 3 * QIN - halo],
        jnp.concatenate([tile[..., 3 * QIN - halo :], after], -1),
    ]
    spread, owner = lax.optimization_barrier((jnp.stack(chunks, 1).reshape(N_DEV, FZ, QIN), owner))
    table = pl.pallas_call(
        assign_kernel,
        out_shape=jax.ShapeDtypeStruct((3, N_DEV), jnp.int32),
        in_specs=[SMEM],
        out_specs=SMEM,
        scratch_shapes=[pltpu.SMEM((N_DEV + 1,), jnp.int32)],
        compiler_params=PARAMS,
        cost_estimate=SMALL,
        name="assign",
    )(owner)
    cut_shape = jax.ShapeDtypeStruct((N_DEV, FZ, CUT), jnp.bfloat16)
    windows, second = pl.pallas_call(
        cut_kernel,
        out_shape=(cut_shape, cut_shape),
        in_specs=[SMEM, SMEM, SMEM, VMEM],
        out_specs=(VMEM, VMEM),
        compiler_params=PARAMS,
        name="cut",
    )(anchor_x, owner, table, exchange(spread))
    lam, back = pl.pallas_call(
        solve_kernel,
        out_shape=(
            jax.ShapeDtypeStruct((3, FZ, LANES), F32),
            jax.ShapeDtypeStruct((N_DEV, FZ, BACK), jnp.bfloat16),
        ),
        in_specs=[SMEM, SMEM, VMEM, VMEM, VMEM, VMEM],
        out_specs=(VMEM, ANY),
        scratch_shapes=[
            *WORK,
            pltpu.VMEM((FZ, LANES), F32),
            pltpu.VMEM((N_DEV, FZ, BACK - 512), jnp.bfloat16),
            MASKS,
            pltpu.SemaphoreType.DMA((5,)),
        ],
        compiler_params=PARAMS,
        name="solve",
    )(me, table, gates, residues, exchange(windows), second)
    back, layers = lax.optimization_barrier((back, conductivity))
    smooth = pl.pallas_call(
        regularize_kernel,
        out_shape=jax.ShapeDtypeStruct(conductivity.shape, F32),
        in_specs=[VMEM],
        out_specs=VMEM,
        compiler_params=PARAMS,
        cost_estimate=SMALL,
        name="regularize",
    )(layers)
    back, smooth = lax.optimization_barrier((exchange(back), smooth))
    columns = pl.pallas_call(
        scatter_kernel,
        out_shape=jax.ShapeDtypeStruct((N_DEV, FZ, 128), F32),
        in_specs=[SMEM, SMEM, VMEM],
        out_specs=VMEM,
        compiler_params=PARAMS,
        name="scatter",
    )(anchor_x, table, back)
    adjoint_field = pl.pallas_call(
        second_kernel,
        out_shape=jax.ShapeDtypeStruct((MOST, 3, FZ, LANES), F32),
        in_specs=[SMEM, SMEM, VMEM, VMEM, VMEM, ANY],
        out_specs=ANY,
        scratch_shapes=[*WORK, MASKS, pltpu.SemaphoreType.DMA((2,))],
        compiler_params=PARAMS,
        cost_estimate=pl.CostEstimate(flops=2 * 10**7, bytes_accessed=4 * 10**6, transcendentals=3 * 10**6),
        name="second",
    )(me, table, gates, residues, back, lam)
    sums, adjoint_field = lax.optimization_barrier((exchange(columns), adjoint_field))
    half = jax.ShapeDtypeStruct((FZ, halo), F32)
    first, own, last = pl.pallas_call(
        join_kernel,
        out_shape=(half, jax.ShapeDtypeStruct((FZ, TX * TY), F32), half),
        in_specs=[VMEM],
        out_specs=(VMEM, VMEM, VMEM),
        compiler_params=PARAMS,
        name="join",
    )(sums)
    from_before, from_after = neighbours(first, last, "row")
    data = own + jnp.pad(from_before, ((0, 0), (0, TX * TY - halo)))
    data = data + jnp.pad(from_after, ((0, 0), (TX * TY - halo, 0)))
    gradient = smooth + jnp.pad(data, ((0, smooth.shape[0] - FZ), (0, 0)))
    return gradient, adjoint_field


def solution(mesh):
    in_specs = (
        P(None, None, ("row", "dev")),
        P(None, ("row", "dev")),
        P("row", None),
        P("row", None),
        P(),
        P("row", None, None),
    )
    out_specs = (P(None, ("row", "dev")), P(("row", "dev"), None, None, None))
    return jax.shard_map(
        per_device, mesh=mesh, in_specs=in_specs, out_specs=out_specs, check_vma=False
    )
```

```python
import jax
import jax.numpy as jnp
from jax import lax
from jax.experimental import pallas as pl
from jax.experimental.pallas import tpu as pltpu
from jax.sharding import PartitionSpec as P

TX = 32
TY = 32
FZ = 40
FP = 48
GATES = 30
NTIMES = 64
STEPS = 2
MOST = 2
FOOT_ROW = 16
HALO = 8
N_DEV = 16
STEP = 0.05

LANES = FP * FP
OWN_ROWS = 8
QIN = 384
CUT = 640
BACK = 896
DEPTH = 48
UNROLL = 8
CUT_UNROLL = 8
LOG2E = 1.4426950408889634
LN15 = 2.70805020110221


def turn(v, by):
    return pltpu.roll(v, by % 128, 1)


def lane_iota(rows):
    return lax.broadcasted_iota(jnp.int32, (rows, 128), 1)


def tall(mask):
    return jnp.concatenate([mask] * (FZ // 8), 0)


def assign(owner, table, seconds):
    for e in range(N_DEV):
        table[0, e] = -1
        table[1, e] = -1
    for f in range(FOOT_ROW):
        e = owner[0, f]
        held, other = table[0, e], table[1, e]
        table[0, e] = jnp.where(held >= 0, held, f)
        table[1, e] = jnp.where(held >= 0, f, other)
    n = jnp.int32(0)
    for e in range(N_DEV):
        other = table[1, e]
        seconds[n] = other
        n = n + (other >= 0).astype(jnp.int32)
    n = jnp.int32(0)
    for e in range(N_DEV):
        held = table[0, e]
        table[2, e] = (held >= 0).astype(jnp.int32)
        table[0, e] = jnp.where(held >= 0, held, seconds[n])
        n = n + (held < 0).astype(jnp.int32)


def tile_kernel(primary, conductivity, out, held, sems):
    copies = [
        pltpu.make_async_copy(primary.at[:, :DEPTH], held.at[:3], sems.at[0]),
        pltpu.make_async_copy(conductivity.at[:DEPTH], held.at[3], sems.at[1]),
    ]
    for copy in copies:
        copy.start()
    for copy in copies:
        copy.wait()
    for c in range(4):
        for q, start in enumerate((768, 896, 0, 128)):
            out[4 * c + q, :, :256] = held[c, :FZ, 256 * q : 256 * q + 256]
            out[4 * c + q, :, 256:] = held[c, :FZ, start : start + 128]


def cut_rows(tiles, o, count):
    d0, s = o // TX, o % TX
    row_in = lane_iota(8) // TX
    made, codes = [], []
    for v in range(-(-FP * count // 128)):
        at = lane_iota(8) + 128 * v
        y = sum((at >= FP * j).astype(jnp.int32) for j in range(1, count + 1))
        codes.append(8 * (y // 4) + y % 4 + 2 * lax.shift_right_logical(at - FP * y + s, 5))
        made.append(jnp.zeros((FZ, 128), jnp.float32))
    for m in range(count // 4):
        tile = [tiles(jnp.minimum(d0 + t, N_DEV - 1), m).astype(jnp.float32) for t in range(3)]
        for n in range(8):
            from_t = [t for t in range(3) if 0 <= n - 2 * t < 4]
            src = tile[from_t[0]]
            for t in from_t[1:]:
                src = jnp.where(tall(row_in == n - 2 * t), tile[t], src)
            turned = turn(src, 192 * m + 16 * n - s)
            rows = [(192 * m + FP * (n - 2 * t), t) for t in from_t]
            for v in range(len(made)):
                if any(
                    at + max(0, TX * t - 31) < 128 * (v + 1) and at + min(FP, TX * (t + 1)) > 128 * v for at, t in rows
                ):
                    made[v] = jnp.where(tall(codes[v] == 8 * m + n), turned, made[v])
    return [v.astype(jnp.bfloat16) for v in made]


def cut_own_kernel(anchor, owner, tiles, out, table, seconds):
    assign(owner, table, seconds)

    def one(e, carry):
        o = anchor[0, table[0, e]]
        made = cut_rows(lambda d, m: tiles[d, :, 128 * m : 128 * m + 128], o, OWN_ROWS)
        for v, lanes in enumerate(made):
            out[e, :, 128 * v : 128 * v + 128] = lanes
        return carry

    lax.fori_loop(0, N_DEV, one, 0, unroll=CUT_UNROLL)


def cut_halo_kernel(anchor, owner, table, tiles, own, out, second):
    def one(e, carry):
        f = table[0, e]
        w = owner[0, f]
        out[e, :, :384] = own[e]
        made = cut_rows(lambda d, m: tiles[d], anchor[0, f], 4)
        out[e, :, 384:512], out[e, :, 512:640] = made
        place = jnp.where(table[1, w] == f, w, N_DEV)
        second[place, :, :384] = own[e]
        second[place, :, 384:512], second[place, :, 512:640] = made
        return carry

    lax.fori_loop(0, N_DEV, one, 0, unroll=CUT_UNROLL)


def adjoint(f, gates, misfit, parts, window, lam, curl, x_masks):
    lam[:, FZ:, :] = jnp.zeros((3, 8, LANES), jnp.float32)
    curl[:, :8, :] = jnp.zeros((3, 8, LANES), jnp.float32)
    x_of = lax.broadcasted_iota(jnp.int32, (8, LANES), 1) % FP
    x_masks[0] = (x_of != FP - 1).astype(jnp.float32)
    x_masks[1] = (x_of != 0).astype(jnp.float32)
    times = 0.1 * jnp.exp((LN15 / (NTIMES - 1)) * gates[...].astype(jnp.float32))
    scaled = -LOG2E * times
    all_lanes = lax.broadcasted_iota(jnp.int32, (8, LANES), 1)
    last_y = all_lanes >= LANES - FP
    first_y = all_lanes < FP

    def ahead_x(v):
        return pltpu.roll(v, LANES - 1, 1) * x_masks[0]

    def behind_x(v):
        return pltpu.roll(v, 1, 1) * x_masks[1]

    def ahead_y(v):
        return jnp.where(last_y, 0.0, pltpu.roll(v, LANES - FP, 1))

    def behind_y(v):
        return jnp.where(first_y, 0.0, pltpu.roll(v, FP, 1))

    low = lane_iota(FZ) < 64
    for c in range(4):
        for q in range(4):
            window[c, :, 384 * q + 384 : 384 * q + 768] = parts[4 * c + q, :, :384].astype(jnp.float32)
        for base, p in ((0, 4 * c), (1920, 4 * c + 2)):
            head, rest = (parts[p, :, n : n + 128].astype(jnp.float32) for n in (384, 512))
            then, last = (turn(parts[p + 1, :, n : n + 128].astype(jnp.float32), 64) for n in (384, 512))
            window[c, :, base : base + 128] = head
            window[c, :, base + 128 : base + 256] = jnp.where(low, rest, then)
            window[c, :, base + 256 : base + 384] = jnp.where(low, then, last)
    residue = misfit[pl.ds(f, 1), :]
    t_of = [jnp.broadcast_to(scaled[:, g : g + 1], (8, 128)) for g in range(GATES)]
    r_of = [jnp.broadcast_to(residue[:, g : g + 1], (8, 128)) for g in range(GATES)]

    def weigh(i, carry):
        z = pl.ds(pl.multiple_of(8 * i, 8), 8)
        for c0 in range(0, LANES, 384):
            at = slice(c0, c0 + 384)
            sigma = window[3, z, at]
            weight = jnp.zeros_like(sigma)
            for g in range(GATES):
                t3 = jnp.concatenate([t_of[g]] * 3, 1)
                r3 = jnp.concatenate([r_of[g]] * 3, 1)
                weight = weight + r3 * jnp.exp2(sigma * t3)
            for c in range(3):
                lam[c, z, at] = weight * window[c, z, at]
        return carry

    lax.fori_loop(0, FZ // 8, weigh, 0)

    def step(n, carry):
        for i in range(FZ // 8):
            z = slice(8 * i, 8 * i + 8)
            up = slice(8 * i + 1, 8 * i + 9)
            vx, vy, vz = lam[0, z, :], lam[1, z, :], lam[2, z, :]
            at = slice(8 * i + 8, 8 * i + 16)
            curl[0, at, :] = (ahead_y(vz) - vz) - (lam[1, up, :] - vy)
            curl[1, at, :] = (lam[0, up, :] - vx) - (ahead_x(vz) - vz)
            curl[2, at, :] = (ahead_x(vy) - vy) - (ahead_y(vx) - vx)
        for i in range(FZ // 8):
            z = slice(8 * i, 8 * i + 8)
            at = slice(8 * i + 8, 8 * i + 16)
            down = slice(8 * i + 7, 8 * i + 15)
            wx, wy, wz = curl[0, at, :], curl[1, at, :], curl[2, at, :]
            ux = (curl[1, down, :] - wy) - (behind_y(wz) - wz)
            uy = (behind_x(wz) - wz) - (curl[0, down, :] - wx)
            uz = (behind_y(wx) - wx) - (behind_x(wy) - wy)
            sigma = window[3, z, :]
            for c, u in enumerate((ux, uy, uz)):
                v = lam[c, z, :]
                lam[c, z, :] = v - STEP * (u + sigma * v)
        return carry

    lax.fori_loop(0, STEPS, step, 0)


def solve_kernel(me, table, gates, misfit, parts, second, lam_out, back, window, lam, curl, local, x_masks):
    f, own = table[0, me[0]], table[2, me[0]]
    adjoint(f, gates, misfit, parts, window, lam, curl, x_masks)
    for i in range(FZ // 8):
        z = slice(8 * i, 8 * i + 8)
        total = None
        for c in range(3):
            v = lam[c, z, :]
            lam_out[c, z, :] = jnp.where(own == 1, v, 0.0)
            term = v * window[c, z, :]
            total = term if total is None else total + term
        local[z, :] = total
    lane = lane_iota(FZ)
    for j in range(N_DEV):

        def taken(base, high_at, rest_at):
            a, r = base // 128, base % 128
            both = [local[:, 128 * g : 128 * g + 128] for g in (a, min(a + 1, LANES // 128 - 1))]
            high = [v.astype(jnp.bfloat16).astype(jnp.float32) for v in both]
            rest = [turn(v - h, rest_at - r) for v, h in zip(both, high)]
            return [turn(h, high_at - r) for h in high], rest, 128 - r

        high, rest, edge = taken(384 + 96 * j, 64, 80)
        halo_high, halo_rest, halo_edge = taken(FP * (j if j < 8 else 32 + j), 32, 48)
        low = second[j, :, 512:640].astype(jnp.float32)
        v4 = jnp.where(lane < 64, low, jnp.where(lane - 64 < edge, high[0], high[1]))
        v5 = jnp.where(lane - 32 < halo_edge, halo_high[0], halo_high[1])
        v5 = jnp.where(lane < 32, jnp.where(lane + 64 < edge, high[0], high[1]), v5)
        v5 = jnp.where(lane < 80, v5, jnp.where(lane - 80 < edge, rest[0], rest[1]))
        v6 = jnp.where(lane - 48 < halo_edge, halo_rest[0], halo_rest[1])
        v6 = jnp.where(lane < 48, jnp.where(lane + 48 < edge, rest[0], rest[1]), v6)
        back[j, :, :512] = second[j, :, :512]
        for b, v in enumerate((v4, v5, v6)):
            back[j, :, 512 + 128 * b : 640 + 128 * b] = v.astype(jnp.bfloat16)


def second_kernel(me, table, gates, misfit, parts, own, adjoint_out, window, lam, curl, x_masks, sems):
    first = pltpu.make_async_copy(own, adjoint_out.at[0], sems.at[0])
    first.start()
    f = table[1, me[0]]

    @pl.when(f >= 0)
    def _():
        adjoint(f, gates, misfit, parts, window, lam, curl, x_masks)

    @pl.when(f < 0)
    def _():
        lam[:, :FZ, :] = jnp.zeros((3, FZ, LANES), jnp.float32)

    copy = pltpu.make_async_copy(lam.at[:, :FZ, :], adjoint_out.at[1], sems.at[1])
    copy.start()
    copy.wait()
    first.wait()


def regularize_kernel(conductivity, out):
    logs = jnp.log(conductivity[...].astype(jnp.float32))
    delta = logs[1:] - logs[:-1]
    zero_row = jnp.zeros_like(logs[:1])
    out[...] = jnp.concatenate([zero_row, delta], 0) - jnp.concatenate([delta, zero_row], 0)


def add_row(out, row, source, at, o):
    lane = lane_iota(FZ)
    g, s = o // 128, o % 128
    turned = turn(source, o - at)
    out[row, g] = out[row, g] + jnp.where((lane >= s) & (lane < s + FP), turned, 0.0)
    out[row, g + 1] = out[row, g + 1] + jnp.where(lane < s + FP - 128, turned, 0.0)


def scatter_halo_kernel(anchor, table, back, out, rows):
    rows[...] = jnp.zeros_like(rows)

    def one(e, carry):
        v5, v6 = (back[e, :, n : n + 128].astype(jnp.float32) for n in (640, 768))
        add_row(rows, 0, v5 + turn(v6, -16), 32, anchor[0, table[0, e]])
        return carry

    lax.fori_loop(0, N_DEV, one, 0, unroll=UNROLL)
    out[...] = rows[0, :4]


def scatter_own_kernel(anchor, table, back, out):
    out[...] = jnp.zeros_like(out)
    lane = lane_iota(FZ)

    def one(e, carry):
        o = anchor[0, table[0, e]]
        v4, v5, v6 = (back[e, :, 512 + 128 * b : 640 + 128 * b].astype(jnp.float32) for b in range(3))
        both = jnp.where(lane >= 64, v4, v5) + turn(jnp.where(lane >= 80, v5, v6), -16)
        add_row(out, 0, both, 64, o)
        add_row(out, 1, both, 112, o)
        return carry

    lax.fori_loop(0, N_DEV, one, 0, unroll=UNROLL)


def collect_kernel(own, halo, out):
    lane_row = lane_iota(FZ) // TX
    for g in range(4):
        rows = [own[0, g], turn(own[1, g], 32), turn(halo[g], 64)]
        for n in range(4):
            v = jnp.where(lane_row == n, rows[0], rows[2])
            out[4 * g + n] = jnp.where(lane_row == (n + 1) % 4, rows[1], v)


def join_kernel(me, sums, smooth, out):
    lane = lane_iota(FZ)
    base = TX * (me[0] % 4)
    made = []
    for v in range(8):
        even, odd = (turn(sums[2 * v + n], 64 * n - base) for n in range(2))
        made.append(jnp.where(lane < 64, even, odd))
    for j in range(N_DEV):
        v = (24 + j) // 4 if j < 8 else (j - 8) // 4
        halo = turn(sums[j], TX * (j % 4) - 64 - base)
        made[v] = made[v] + jnp.where(lane // TX == j % 4, halo, 0.0)
    for v in range(8):
        at = slice(128 * v, 128 * v + 128)
        out[:FZ, at] = smooth[:FZ, at] + made[v]
    out[FZ:, :] = smooth[FZ:, :]


def to_neighbours(array, goes_up):
    bands, width = lax.axis_size("row"), lax.axis_size("dev")
    pairs = []
    for r in range(bands):
        for d in range(width):
            other = r + 1 if goes_up(d) else r - 1
            if 0 <= other < bands:
                pairs.append((r * width + d, other * width + d))
    return lax.ppermute(array, ("row", "dev"), pairs)


SMEM = pl.BlockSpec(memory_space=pltpu.SMEM)
VMEM = pl.BlockSpec(memory_space=pltpu.VMEM)
ANY = pl.BlockSpec(memory_space=pl.ANY)
PARAMS = pltpu.CompilerParams(vmem_limit_bytes=24 * 2**20)
F32 = jnp.float32
WIDE = 64 * 2**20 - 640 * 2**10
SMALL = pl.CostEstimate(flops=10**6, bytes_accessed=10**6, transcendentals=10**5)
WORK = [
    pltpu.VMEM((4, FZ, LANES), F32),
    pltpu.VMEM((3, FZ + 8, LANES), F32),
    pltpu.VMEM((3, FZ + 8, LANES), F32),
]
MASKS = pltpu.VMEM((2, 8, LANES), F32)


def exchange(blocks):
    return lax.all_to_all(blocks, "dev", 0, 0, tiled=True)


def per_device(primary, conductivity, anchor_x, owner, gate_index, misfit):
    me = lax.axis_index("dev").astype(jnp.int32).reshape(1)
    gates, residues = gate_index.reshape(1, GATES), misfit[0]
    spread = pl.pallas_call(
        tile_kernel,
        out_shape=jax.ShapeDtypeStruct((N_DEV, FZ, QIN), jnp.bfloat16),
        in_specs=[ANY, ANY],
        out_specs=VMEM,
        scratch_shapes=[pltpu.VMEM((4, DEPTH, TX * TY), jnp.bfloat16), pltpu.SemaphoreType.DMA((2,))],
        compiler_params=pltpu.CompilerParams(vmem_limit_bytes=WIDE),
        name="tile",
    )(primary, conductivity)
    tiles = exchange(spread)
    halo_tiles = to_neighbours(tiles[:, :, 256:], lambda d: d % 4 < 2)
    own_cut, table = pl.pallas_call(
        cut_own_kernel,
        out_shape=(
            jax.ShapeDtypeStruct((N_DEV, FZ, 384), jnp.bfloat16),
            jax.ShapeDtypeStruct((3, N_DEV), jnp.int32),
        ),
        in_specs=[SMEM, SMEM, VMEM],
        out_specs=(VMEM, SMEM),
        scratch_shapes=[pltpu.SMEM((N_DEV + 1,), jnp.int32)],
        compiler_params=PARAMS,
        cost_estimate=SMALL,
        name="cut_own",
    )(anchor_x, owner, tiles)
    cut_shape = jax.ShapeDtypeStruct((N_DEV, FZ, CUT), jnp.bfloat16)
    windows, second = pl.pallas_call(
        cut_halo_kernel,
        out_shape=(cut_shape, jax.ShapeDtypeStruct((N_DEV + 1, FZ, CUT), jnp.bfloat16)),
        in_specs=[SMEM, SMEM, SMEM, VMEM, VMEM],
        out_specs=(VMEM, VMEM),
        compiler_params=PARAMS,
        name="cut_halo",
    )(anchor_x, owner, table, halo_tiles, own_cut)
    windows, layers = lax.optimization_barrier((windows, conductivity))
    smooth = pl.pallas_call(
        regularize_kernel,
        out_shape=jax.ShapeDtypeStruct(conductivity.shape, F32),
        in_specs=[VMEM],
        out_specs=VMEM,
        compiler_params=PARAMS,
        cost_estimate=SMALL,
        name="regularize",
    )(layers)
    parts, smooth = lax.optimization_barrier((exchange(windows), smooth))
    lam, back = pl.pallas_call(
        solve_kernel,
        out_shape=(
            jax.ShapeDtypeStruct((3, FZ, LANES), F32),
            jax.ShapeDtypeStruct((N_DEV, FZ, BACK), jnp.bfloat16),
        ),
        in_specs=[SMEM, SMEM, VMEM, VMEM, VMEM, VMEM],
        out_specs=(VMEM, VMEM),
        scratch_shapes=[*WORK, pltpu.VMEM((FZ, LANES), F32), MASKS],
        compiler_params=PARAMS,
        name="solve",
    )(me, table, gates, residues, parts, second)
    back = exchange(back)
    halo_rows = pl.pallas_call(
        scatter_halo_kernel,
        out_shape=jax.ShapeDtypeStruct((4, FZ, 128), F32),
        in_specs=[SMEM, SMEM, VMEM],
        out_specs=VMEM,
        scratch_shapes=[pltpu.VMEM((1, 5, FZ, 128), F32)],
        compiler_params=PARAMS,
        name="scatter_halo",
    )(anchor_x, table, back)
    halo_rows, sums = lax.optimization_barrier((halo_rows, back))
    halo_rows = to_neighbours(halo_rows, lambda d: d >= 8)
    own_rows = pl.pallas_call(
        scatter_own_kernel,
        out_shape=jax.ShapeDtypeStruct((2, 5, FZ, 128), F32),
        in_specs=[SMEM, SMEM, VMEM],
        out_specs=VMEM,
        compiler_params=PARAMS,
        cost_estimate=SMALL,
        name="scatter_own",
    )(anchor_x, table, sums)
    columns = pl.pallas_call(
        collect_kernel,
        out_shape=jax.ShapeDtypeStruct((N_DEV, FZ, 128), F32),
        in_specs=[VMEM, VMEM],
        out_specs=VMEM,
        compiler_params=PARAMS,
        name="collect",
    )(own_rows, halo_rows)
    columns, back = lax.optimization_barrier((columns, back))
    adjoint_field = pl.pallas_call(
        second_kernel,
        out_shape=jax.ShapeDtypeStruct((MOST, 3, FZ, LANES), F32),
        in_specs=[SMEM, SMEM, VMEM, VMEM, VMEM, ANY],
        out_specs=ANY,
        scratch_shapes=[*WORK, MASKS, pltpu.SemaphoreType.DMA((2,))],
        compiler_params=PARAMS,
        cost_estimate=pl.CostEstimate(flops=2 * 10**7, bytes_accessed=4 * 10**6, transcendentals=3 * 10**6),
        name="second",
    )(me, table, gates, residues, back, lam)
    columns, adjoint_field = lax.optimization_barrier((exchange(columns), adjoint_field))
    gradient = pl.pallas_call(
        join_kernel,
        out_shape=jax.ShapeDtypeStruct(conductivity.shape, F32),
        in_specs=[SMEM, VMEM, VMEM],
        out_specs=VMEM,
        compiler_params=PARAMS,
        name="join",
    )(me, columns, smooth)
    return gradient, adjoint_field


def solution(mesh):
    in_specs = (
        P(None, None, ("row", "dev")),
        P(None, ("row", "dev")),
        P("row", None),
        P("row", None),
        P(),
        P("row", None, None),
    )
    out_specs = (P(None, ("row", "dev")), P(("row", "dev"), None, None, None))
    return jax.shard_map(
        per_device, mesh=mesh, in_specs=in_specs, out_specs=out_specs, check_vma=False
    )
```

```python
import jax
import jax.numpy as jnp
from jax import lax
from jax.experimental import pallas as pl
from jax.experimental.pallas import tpu as pltpu
from jax.sharding import PartitionSpec as P

TX = 32
TY = 32
FZ = 40
FP = 48
GATES = 30
NTIMES = 64
STEPS = 2
MOST = 2
FOOT_ROW = 16
N_DEV = 16
STEP = 0.05

LANES = FP * FP
OWN_ROWS = 8
QIN = 384
CUT = 640
BACK = 896
DEPTH = 48
UNROLL = 8
CUT_UNROLL = 8
LOG2E = 1.4426950408889634
LN15 = 2.70805020110221


def turn(v, by):
    return pltpu.roll(v, by % 128, 1)


def lane_iota(rows):
    return lax.broadcasted_iota(jnp.int32, (rows, 128), 1)


def tall(mask):
    return jnp.concatenate([mask] * (FZ // 8), 0)


def assign(owner, table, seconds):
    for e in range(N_DEV):
        table[0, e] = -1
        table[1, e] = -1
    for f in range(FOOT_ROW):
        e = owner[0, f]
        held, other = table[0, e], table[1, e]
        table[0, e] = jnp.where(held >= 0, held, f)
        table[1, e] = jnp.where(held >= 0, f, other)
    n = jnp.int32(0)
    for e in range(N_DEV):
        other = table[1, e]
        seconds[n] = other
        n = n + (other >= 0).astype(jnp.int32)
    n = jnp.int32(0)
    for e in range(N_DEV):
        held = table[0, e]
        table[2, e] = (held >= 0).astype(jnp.int32)
        table[0, e] = jnp.where(held >= 0, held, seconds[n])
        n = n + (held < 0).astype(jnp.int32)


def tile_kernel(primary, conductivity, out_to, held, out, sems):
    arrivals = [pltpu.make_async_copy(primary.at[c, :DEPTH], held.at[c], sems.at[0, c]) for c in range(3)]
    arrivals.append(pltpu.make_async_copy(conductivity.at[:DEPTH], held.at[3], sems.at[0, 3]))
    for copy in arrivals:
        copy.start()
    leaving = []
    for c in range(4):
        arrivals[c].wait()
        for q, start in enumerate((768, 896, 0, 128)):
            out[4 * c + q, :, :256] = held[c, :FZ, 256 * q : 256 * q + 256]
            out[4 * c + q, :, 256:] = held[c, :FZ, start : start + 128]
        some = slice(4 * c, 4 * c + 4)
        leaving.append(pltpu.make_async_copy(out.at[some], out_to.at[some], sems.at[1, c]))
        leaving[-1].start()
    for copy in leaving:
        copy.wait()


def cut_rows(tiles, o, count):
    d0, s = o // TX, o % TX
    row_in = lane_iota(8) // TX
    made, codes = [], []
    for v in range(-(-FP * count // 128)):
        at = lane_iota(8) + 128 * v
        y = sum((at >= FP * j).astype(jnp.int32) for j in range(1, count + 1))
        codes.append(8 * (y // 4) + y % 4 + 2 * lax.shift_right_logical(at - FP * y + s, 5))
        made.append(jnp.zeros((FZ, 128), jnp.float32))
    for m in range(count // 4):
        tile = [tiles(jnp.minimum(d0 + t, N_DEV - 1), m).astype(jnp.float32) for t in range(3)]
        for n in range(8):
            from_t = [t for t in range(3) if 0 <= n - 2 * t < 4]
            src = tile[from_t[0]]
            for t in from_t[1:]:
                src = jnp.where(tall(row_in == n - 2 * t), tile[t], src)
            turned = turn(src, 192 * m + 16 * n - s)
            rows = [(192 * m + FP * (n - 2 * t), t) for t in from_t]
            for v in range(len(made)):
                if any(
                    at + max(0, TX * t - 31) < 128 * (v + 1) and at + min(FP, TX * (t + 1)) > 128 * v for at, t in rows
                ):
                    made[v] = jnp.where(tall(codes[v] == 8 * m + n), turned, made[v])
    return [v.astype(jnp.bfloat16) for v in made]


def in_halves(one, copy_of):
    half = N_DEV // 2
    copies = [copy_of(h, slice(half * h, half * h + half)) for h in range(2)]
    for h, copy in enumerate(copies):
        lax.fori_loop(half * h, half * h + half, one, 0, unroll=CUT_UNROLL)
        copy.start()
    for copy in copies:
        copy.wait()


def cut_own_kernel(anchor, owner, tiles, out, windows, table, seconds, sems):
    assign(owner, table, seconds)

    def one(e, carry):
        o = anchor[0, table[0, e]]
        made = cut_rows(lambda d, m: tiles[d, :, 128 * m : 128 * m + 128], o, OWN_ROWS)
        for v, lanes in enumerate(made):
            out[e, :, 128 * v : 128 * v + 128] = lanes
        return carry

    in_halves(one, lambda h, at: pltpu.make_async_copy(out.at[at], windows.at[at, :, :384], sems.at[h]))


def cut_halo_kernel(anchor, owner, table, tiles, own, windows_in, windows, second, out, sems):
    del windows_in

    def one(e, carry):
        f = table[0, e]
        w = owner[0, f]
        made = cut_rows(lambda d, m: tiles[d], anchor[0, f], 4)
        out[e, :, :128], out[e, :, 128:] = made
        place = jnp.where(table[1, w] == f, w, N_DEV)
        second[place, :, :384] = own[e]
        second[place, :, 384:512], second[place, :, 512:640] = made
        return carry

    in_halves(one, lambda h, at: pltpu.make_async_copy(out.at[at], windows.at[at, :, 384:], sems.at[h]))


def adjoint(f, gates, misfit, parts, window, lam, curl, x_masks):
    lam[:, FZ:, :] = jnp.zeros((3, 8, LANES), jnp.float32)
    curl[:, :8, :] = jnp.zeros((3, 8, LANES), jnp.float32)
    x_of = lax.broadcasted_iota(jnp.int32, (8, LANES), 1) % FP
    x_masks[0] = (x_of != FP - 1).astype(jnp.float32)
    x_masks[1] = (x_of != 0).astype(jnp.float32)
    times = 0.1 * jnp.exp((LN15 / (NTIMES - 1)) * gates[...].astype(jnp.float32))
    scaled = -LOG2E * times
    all_lanes = lax.broadcasted_iota(jnp.int32, (8, LANES), 1)
    last_y = all_lanes >= LANES - FP
    first_y = all_lanes < FP

    def ahead_x(v):
        return pltpu.roll(v, LANES - 1, 1) * x_masks[0]

    def behind_x(v):
        return pltpu.roll(v, 1, 1) * x_masks[1]

    def ahead_y(v):
        return jnp.where(last_y, 0.0, pltpu.roll(v, LANES - FP, 1))

    def behind_y(v):
        return jnp.where(first_y, 0.0, pltpu.roll(v, FP, 1))

    low = lane_iota(FZ) < 64
    for c in range(4):
        for q in range(4):
            window[c, :, 384 * q + 384 : 384 * q + 768] = parts[4 * c + q, :, :384].astype(jnp.float32)
        for base, p in ((0, 4 * c), (1920, 4 * c + 2)):
            head, rest = (parts[p, :, n : n + 128].astype(jnp.float32) for n in (384, 512))
            then, last = (turn(parts[p + 1, :, n : n + 128].astype(jnp.float32), 64) for n in (384, 512))
            window[c, :, base : base + 128] = head
            window[c, :, base + 128 : base + 256] = jnp.where(low, rest, then)
            window[c, :, base + 256 : base + 384] = jnp.where(low, then, last)
    residue = misfit[pl.ds(f, 1), :]
    t_of = [jnp.broadcast_to(scaled[:, g : g + 1], (8, 128)) for g in range(GATES)]
    r_of = [jnp.broadcast_to(residue[:, g : g + 1], (8, 128)) for g in range(GATES)]

    def weigh(i, carry):
        z = pl.ds(pl.multiple_of(8 * i, 8), 8)
        for c0 in range(0, LANES, 384):
            at = slice(c0, c0 + 384)
            sigma = window[3, z, at]
            weight = jnp.zeros_like(sigma)
            for g in range(GATES):
                t3 = jnp.concatenate([t_of[g]] * 3, 1)
                r3 = jnp.concatenate([r_of[g]] * 3, 1)
                weight = weight + r3 * jnp.exp2(sigma * t3)
            for c in range(3):
                lam[c, z, at] = weight * window[c, z, at]
        return carry

    lax.fori_loop(0, FZ // 8, weigh, 0)

    def step(n, carry):
        for i in range(FZ // 8):
            z = slice(8 * i, 8 * i + 8)
            up = slice(8 * i + 1, 8 * i + 9)
            vx, vy, vz = lam[0, z, :], lam[1, z, :], lam[2, z, :]
            at = slice(8 * i + 8, 8 * i + 16)
            curl[0, at, :] = (ahead_y(vz) - vz) - (lam[1, up, :] - vy)
            curl[1, at, :] = (lam[0, up, :] - vx) - (ahead_x(vz) - vz)
            curl[2, at, :] = (ahead_x(vy) - vy) - (ahead_y(vx) - vx)
        for i in range(FZ // 8):
            z = slice(8 * i, 8 * i + 8)
            at = slice(8 * i + 8, 8 * i + 16)
            down = slice(8 * i + 7, 8 * i + 15)
            wx, wy, wz = curl[0, at, :], curl[1, at, :], curl[2, at, :]
            ux = (curl[1, down, :] - wy) - (behind_y(wz) - wz)
            uy = (behind_x(wz) - wz) - (curl[0, down, :] - wx)
            uz = (behind_y(wx) - wx) - (behind_x(wy) - wy)
            sigma = window[3, z, :]
            for c, u in enumerate((ux, uy, uz)):
                v = lam[c, z, :]
                lam[c, z, :] = v - STEP * (u + sigma * v)
        return carry

    lax.fori_loop(0, STEPS, step, 0)


def solve_kernel(me, table, gates, misfit, parts, second, lam_out, back, window, lam, curl, local, x_masks):
    f, own = table[0, me[0]], table[2, me[0]]
    adjoint(f, gates, misfit, parts, window, lam, curl, x_masks)
    for i in range(FZ // 8):
        z = slice(8 * i, 8 * i + 8)
        total = None
        for c in range(3):
            v = lam[c, z, :]
            lam_out[c, z, :] = jnp.where(own == 1, v, 0.0)
            term = v * window[c, z, :]
            total = term if total is None else total + term
        local[z, :] = total
    lane = lane_iota(FZ)
    for j in range(N_DEV):

        def taken(base, high_at, rest_at):
            a, r = base // 128, base % 128
            both = [local[:, 128 * g : 128 * g + 128] for g in (a, min(a + 1, LANES // 128 - 1))]
            high = [v.astype(jnp.bfloat16).astype(jnp.float32) for v in both]
            rest = [turn(v - h, rest_at - r) for v, h in zip(both, high)]
            return [turn(h, high_at - r) for h in high], rest, 128 - r

        high, rest, edge = taken(384 + 96 * j, 64, 80)
        halo_high, halo_rest, halo_edge = taken(FP * (j if j < 8 else 32 + j), 32, 48)
        low = second[j, :, 512:640].astype(jnp.float32)
        v4 = jnp.where(lane < 64, low, jnp.where(lane - 64 < edge, high[0], high[1]))
        v5 = jnp.where(lane - 32 < halo_edge, halo_high[0], halo_high[1])
        v5 = jnp.where(lane < 32, jnp.where(lane + 64 < edge, high[0], high[1]), v5)
        v5 = jnp.where(lane < 80, v5, jnp.where(lane - 80 < edge, rest[0], rest[1]))
        v6 = jnp.where(lane - 48 < halo_edge, halo_rest[0], halo_rest[1])
        v6 = jnp.where(lane < 48, jnp.where(lane + 48 < edge, rest[0], rest[1]), v6)
        back[j, :, :512] = second[j, :, :512]
        for b, v in enumerate((v4, v5, v6)):
            back[j, :, 512 + 128 * b : 640 + 128 * b] = v.astype(jnp.bfloat16)


def second_kernel(me, table, gates, misfit, parts, own, adjoint_out, window, lam, curl, x_masks, sems):
    first = pltpu.make_async_copy(own, adjoint_out.at[0], sems.at[0])
    first.start()
    f = table[1, me[0]]

    @pl.when(f >= 0)
    def _():
        adjoint(f, gates, misfit, parts, window, lam, curl, x_masks)

    @pl.when(f < 0)
    def _():
        lam[:, :FZ, :] = jnp.zeros((3, FZ, LANES), jnp.float32)

    copy = pltpu.make_async_copy(lam.at[:, :FZ, :], adjoint_out.at[1], sems.at[1])
    copy.start()
    copy.wait()
    first.wait()


def regularize_kernel(conductivity, out):
    logs = jnp.log(conductivity[...].astype(jnp.float32))
    delta = logs[1:] - logs[:-1]
    zero_row = jnp.zeros_like(logs[:1])
    out[...] = jnp.concatenate([zero_row, delta], 0) - jnp.concatenate([delta, zero_row], 0)


def add_row(out, row, source, at, o):
    lane = lane_iota(FZ)
    g, s = o // 128, o % 128
    turned = turn(source, o - at)
    out[row, g] = out[row, g] + jnp.where((lane >= s) & (lane < s + FP), turned, 0.0)
    out[row, g + 1] = out[row, g + 1] + jnp.where(lane < s + FP - 128, turned, 0.0)


def scatter_halo_kernel(anchor, table, back, out, rows):
    rows[...] = jnp.zeros_like(rows)

    def one(e, carry):
        v5, v6 = (back[e, :, n : n + 128].astype(jnp.float32) for n in (640, 768))
        add_row(rows, 0, v5 + turn(v6, -16), 32, anchor[0, table[0, e]])
        return carry

    lax.fori_loop(0, N_DEV, one, 0, unroll=UNROLL)
    out[...] = rows[0, :4]


def scatter_own_kernel(anchor, table, back, out):
    out[...] = jnp.zeros_like(out)
    lane = lane_iota(FZ)

    def one(e, carry):
        o = anchor[0, table[0, e]]
        v4, v5, v6 = (back[e, :, 512 + 128 * b : 640 + 128 * b].astype(jnp.float32) for b in range(3))
        both = jnp.where(lane >= 64, v4, v5) + turn(jnp.where(lane >= 80, v5, v6), -16)
        add_row(out, 0, both, 64, o)
        add_row(out, 1, both, 112, o)
        return carry

    lax.fori_loop(0, N_DEV, one, 0, unroll=UNROLL)


def collect_kernel(own, halo, out):
    lane_row = lane_iota(32) // TX
    for g in range(4):
        whole = (own[0, g], own[1, g], halo[g])
        rows = [turn(v[:32], 32 * n) for n, v in enumerate(whole)]
        deep = jnp.concatenate([turn(v[32:], 96) for v in whole] + [jnp.zeros((8, 128), jnp.float32)], 0)
        for n in range(4):
            v = jnp.where(lane_row == n, rows[0], deep)
            for m in range(1, 3):
                v = jnp.where(lane_row == (n + m) % 4, rows[m], v)
            out[4 * g + n] = v


def join_kernel(me, sums, smooth, out):
    lane = lane_iota(FZ)
    base = TX * (me[0] % 4)
    made = []
    for v in range(8):
        halves = []
        for n in range(2):
            top = turn(sums[2 * v + n], 64 * n - base)
            even, odd = (turn(sums[2 * v + n, 8 * m : 8 * m + 8], 64 * n + 32 + 32 * m - base) for m in range(2))
            halves.append(jnp.concatenate([top, jnp.where(lane[:8] % 64 < TX, even, odd)], 0))
        made.append(jnp.where(lane < 64, halves[0], halves[1]))
    for j in range(N_DEV):
        v = (24 + j) // 4 if j < 8 else (j - 8) // 4
        at = TX * (j % 4) - base
        halo = jnp.concatenate([turn(sums[j], at - 64), turn(sums[j, 16:24], at - 96)], 0)
        made[v] = made[v] + jnp.where(lane // TX == j % 4, halo, 0.0)
    for v in range(8):
        at = slice(128 * v, 128 * v + 128)
        out[:FZ, at] = smooth[:FZ, at] + made[v]
    out[FZ:, :] = smooth[FZ:, :]


def to_neighbours(array, goes_up):
    bands, width = lax.axis_size("row"), lax.axis_size("dev")
    pairs = []
    for r in range(bands):
        for d in range(width):
            other = r + 1 if goes_up(d) else r - 1
            if 0 <= other < bands:
                pairs.append((r * width + d, other * width + d))
    return lax.ppermute(array, ("row", "dev"), pairs)


SMEM = pl.BlockSpec(memory_space=pltpu.SMEM)
VMEM = pl.BlockSpec(memory_space=pltpu.VMEM)
ANY = pl.BlockSpec(memory_space=pl.ANY)
PARAMS = pltpu.CompilerParams(vmem_limit_bytes=24 * 2**20)
F32 = jnp.float32
WIDE = 64 * 2**20 - 640 * 2**10
SMALL = pl.CostEstimate(flops=10**6, bytes_accessed=10**6, transcendentals=10**5)
WORK = [
    pltpu.VMEM((4, FZ, LANES), F32),
    pltpu.VMEM((3, FZ + 8, LANES), F32),
    pltpu.VMEM((3, FZ + 8, LANES), F32),
]
MASKS = pltpu.VMEM((2, 8, LANES), F32)


def exchange(blocks):
    return lax.all_to_all(blocks, "dev", 0, 0, tiled=True)


def per_device(primary, conductivity, anchor_x, owner, gate_index, misfit):
    me = lax.axis_index("dev").astype(jnp.int32).reshape(1)
    gates, residues = gate_index.reshape(1, GATES), misfit[0]
    spread = pl.pallas_call(
        tile_kernel,
        out_shape=jax.ShapeDtypeStruct((N_DEV, FZ, QIN), jnp.bfloat16),
        in_specs=[ANY, ANY],
        out_specs=ANY,
        scratch_shapes=[
            pltpu.VMEM((4, DEPTH, TX * TY), jnp.bfloat16),
            pltpu.VMEM((N_DEV, FZ, QIN), jnp.bfloat16),
            pltpu.SemaphoreType.DMA((2, 4)),
        ],
        compiler_params=pltpu.CompilerParams(vmem_limit_bytes=WIDE),
        name="tile",
    )(primary, conductivity)
    tiles = exchange(spread)
    halo_tiles = to_neighbours(tiles[:, :, 256:], lambda d: d % 4 < 2)
    cut_shape = jax.ShapeDtypeStruct((N_DEV, FZ, CUT), jnp.bfloat16)
    own_cut, windows, table = pl.pallas_call(
        cut_own_kernel,
        out_shape=(
            jax.ShapeDtypeStruct((N_DEV, FZ, 384), jnp.bfloat16),
            cut_shape,
            jax.ShapeDtypeStruct((3, N_DEV), jnp.int32),
        ),
        in_specs=[SMEM, SMEM, VMEM],
        out_specs=(VMEM, ANY, SMEM),
        scratch_shapes=[pltpu.SMEM((N_DEV + 1,), jnp.int32), pltpu.SemaphoreType.DMA((2,))],
        compiler_params=PARAMS,
        cost_estimate=SMALL,
        name="cut_own",
    )(anchor_x, owner, tiles)
    windows, second = pl.pallas_call(
        cut_halo_kernel,
        out_shape=(cut_shape, jax.ShapeDtypeStruct((N_DEV + 1, FZ, CUT), jnp.bfloat16)),
        in_specs=[SMEM, SMEM, SMEM, VMEM, VMEM, ANY],
        out_specs=(ANY, VMEM),
        scratch_shapes=[pltpu.VMEM((N_DEV, FZ, CUT - 384), jnp.bfloat16), pltpu.SemaphoreType.DMA((2,))],
        input_output_aliases={5: 0},
        compiler_params=PARAMS,
        name="cut_halo",
    )(anchor_x, owner, table, halo_tiles, own_cut, windows)
    windows, layers = lax.optimization_barrier((windows, conductivity))
    smooth = pl.pallas_call(
        regularize_kernel,
        out_shape=jax.ShapeDtypeStruct(conductivity.shape, F32),
        in_specs=[VMEM],
        out_specs=VMEM,
        compiler_params=PARAMS,
        cost_estimate=SMALL,
        name="regularize",
    )(layers)
    parts, smooth = lax.optimization_barrier((exchange(windows), smooth))
    lam, back = pl.pallas_call(
        solve_kernel,
        out_shape=(
            jax.ShapeDtypeStruct((3, FZ, LANES), F32),
            jax.ShapeDtypeStruct((N_DEV, FZ, BACK), jnp.bfloat16),
        ),
        in_specs=[SMEM, SMEM, VMEM, VMEM, VMEM, VMEM],
        out_specs=(VMEM, VMEM),
        scratch_shapes=[*WORK, pltpu.VMEM((FZ, LANES), F32), MASKS],
        compiler_params=PARAMS,
        name="solve",
    )(me, table, gates, residues, parts, second)
    back = exchange(back)
    halo_rows = pl.pallas_call(
        scatter_halo_kernel,
        out_shape=jax.ShapeDtypeStruct((4, FZ, 128), F32),
        in_specs=[SMEM, SMEM, VMEM],
        out_specs=VMEM,
        scratch_shapes=[pltpu.VMEM((1, 5, FZ, 128), F32)],
        compiler_params=PARAMS,
        name="scatter_halo",
    )(anchor_x, table, back)
    halo_rows, sums = lax.optimization_barrier((halo_rows, back))
    halo_rows = to_neighbours(halo_rows, lambda d: d >= 8)
    own_rows = pl.pallas_call(
        scatter_own_kernel,
        out_shape=jax.ShapeDtypeStruct((2, 5, FZ, 128), F32),
        in_specs=[SMEM, SMEM, VMEM],
        out_specs=VMEM,
        compiler_params=PARAMS,
        cost_estimate=SMALL,
        name="scatter_own",
    )(anchor_x, table, sums)
    columns = pl.pallas_call(
        collect_kernel,
        out_shape=jax.ShapeDtypeStruct((N_DEV, 32, 128), F32),
        in_specs=[VMEM, VMEM],
        out_specs=VMEM,
        compiler_params=PARAMS,
        name="collect",
    )(own_rows, halo_rows)
    columns, back = lax.optimization_barrier((columns, back))
    adjoint_field = pl.pallas_call(
        second_kernel,
        out_shape=jax.ShapeDtypeStruct((MOST, 3, FZ, LANES), F32),
        in_specs=[SMEM, SMEM, VMEM, VMEM, VMEM, ANY],
        out_specs=ANY,
        scratch_shapes=[*WORK, MASKS, pltpu.SemaphoreType.DMA((2,))],
        compiler_params=PARAMS,
        cost_estimate=pl.CostEstimate(flops=2 * 10**7, bytes_accessed=4 * 10**6, transcendentals=3 * 10**6),
        name="second",
    )(me, table, gates, residues, back, lam)
    columns, adjoint_field = lax.optimization_barrier((exchange(columns), adjoint_field))
    gradient = pl.pallas_call(
        join_kernel,
        out_shape=jax.ShapeDtypeStruct(conductivity.shape, F32),
        in_specs=[SMEM, VMEM, VMEM],
        out_specs=VMEM,
        compiler_params=PARAMS,
        name="join",
    )(me, columns, smooth)
    return gradient, adjoint_field


def solution(mesh):
    in_specs = (
        P(None, None, ("row", "dev")),
        P(None, ("row", "dev")),
        P("row", None),
        P("row", None),
        P(),
        P("row", None, None),
    )
    out_specs = (P(None, ("row", "dev")), P(("row", "dev"), None, None, None))
    return jax.shard_map(
        per_device, mesh=mesh, in_specs=in_specs, out_specs=out_specs, check_vma=False
    )
```

```python
import jax
import jax.numpy as jnp
from jax import lax
from jax.experimental import pallas as pl
from jax.experimental.pallas import tpu as pltpu
from jax.sharding import PartitionSpec as P

TX = 32
TY = 32
FZ = 40
FP = 48
GATES = 30
NTIMES = 64
STEPS = 2
MOST = 2
FOOT_ROW = 16
N_DEV = 16
STEP = 0.05

LANES = FP * FP
OWN_ROWS = 8
QIN = 384
CUT = 640
BACK = 896
DEPTH = 48
UNROLL = 8
CUT_UNROLL = 8
LOG2E = 1.4426950408889634
LN15 = 2.70805020110221


def turn(v, by):
    return pltpu.roll(v, by % 128, 1)


def lane_iota(rows):
    return lax.broadcasted_iota(jnp.int32, (rows, 128), 1)


def tall(mask):
    return jnp.concatenate([mask] * (FZ // 8), 0)


def assign(owner, table, seconds):
    for e in range(N_DEV):
        table[0, e] = -1
        table[1, e] = -1
    for f in range(FOOT_ROW):
        e = owner[0, f]
        held, other = table[0, e], table[1, e]
        table[0, e] = jnp.where(held >= 0, held, f)
        table[1, e] = jnp.where(held >= 0, f, other)
    n = jnp.int32(0)
    for e in range(N_DEV):
        other = table[1, e]
        seconds[n] = other
        n = n + (other >= 0).astype(jnp.int32)
    n = jnp.int32(0)
    for e in range(N_DEV):
        held = table[0, e]
        table[2, e] = (held >= 0).astype(jnp.int32)
        table[0, e] = jnp.where(held >= 0, held, seconds[n])
        n = n + (held < 0).astype(jnp.int32)


def tile_kernel(primary, conductivity, out_to, held, out, sems):
    arrivals = [pltpu.make_async_copy(primary.at[c, :DEPTH], held.at[c], sems.at[0, c]) for c in range(3)]
    arrivals.append(pltpu.make_async_copy(conductivity.at[:DEPTH], held.at[3], sems.at[0, 3]))
    for copy in arrivals:
        copy.start()
    leaving = []
    for c in range(4):
        arrivals[c].wait()
        for q, start in enumerate((768, 896, 0, 128)):
            out[4 * c + q, :, :256] = held[c, :FZ, 256 * q : 256 * q + 256]
            out[4 * c + q, :, 256:] = held[c, :FZ, start : start + 128]
        some = slice(4 * c, 4 * c + 4)
        leaving.append(pltpu.make_async_copy(out.at[some], out_to.at[some], sems.at[1, c]))
        leaving[-1].start()
    for copy in leaving:
        copy.wait()


def cut_rows(tiles, o, count):
    d0, s = o // TX, o % TX
    row_in = lane_iota(8) // TX
    made, codes = [], []
    for v in range(-(-FP * count // 128)):
        at = lane_iota(8) + 128 * v
        y = sum((at >= FP * j).astype(jnp.int32) for j in range(1, count + 1))
        codes.append(8 * (y // 4) + y % 4 + 2 * lax.shift_right_logical(at - FP * y + s, 5))
        made.append(jnp.zeros((FZ, 128), jnp.float32))
    for m in range(count // 4):
        tile = [tiles(jnp.minimum(d0 + t, N_DEV - 1), m).astype(jnp.float32) for t in range(3)]
        for n in range(8):
            from_t = [t for t in range(3) if 0 <= n - 2 * t < 4]
            src = tile[from_t[0]]
            for t in from_t[1:]:
                src = jnp.where(tall(row_in == n - 2 * t), tile[t], src)
            turned = turn(src, 192 * m + 16 * n - s)
            rows = [(192 * m + FP * (n - 2 * t), t) for t in from_t]
            for v in range(len(made)):
                if any(
                    at + max(0, TX * t - 31) < 128 * (v + 1) and at + min(FP, TX * (t + 1)) > 128 * v for at, t in rows
                ):
                    made[v] = jnp.where(tall(codes[v] == 8 * m + n), turned, made[v])
    return [v.astype(jnp.bfloat16) for v in made]


def in_halves(one, copy_of):
    half = N_DEV // 2
    copies = [copy_of(h, slice(half * h, half * h + half)) for h in range(2)]
    for h, copy in enumerate(copies):
        lax.fori_loop(half * h, half * h + half, one, 0, unroll=CUT_UNROLL)
        copy.start()
    for copy in copies:
        copy.wait()


def cut_own_kernel(anchor, owner, tiles, out, windows, table, seconds, sems):
    assign(owner, table, seconds)

    def one(e, carry):
        o = anchor[0, table[0, e]]
        made = cut_rows(lambda d, m: tiles[d, :, 128 * m : 128 * m + 128], o, OWN_ROWS)
        for v, lanes in enumerate(made):
            out[e, :, 128 * v : 128 * v + 128] = lanes
        return carry

    in_halves(one, lambda h, at: pltpu.make_async_copy(out.at[at], windows.at[at, :, :384], sems.at[h]))


def cut_halo_kernel(anchor, owner, table, tiles, own, windows_in, windows, second, out, sems):
    del windows_in

    def one(e, carry):
        f = table[0, e]
        w = owner[0, f]
        made = cut_rows(lambda d, m: tiles[d], anchor[0, f], 4)
        out[e, :, :128], out[e, :, 128:] = made
        place = jnp.where(table[1, w] == f, w, N_DEV)
        second[place, :, :384] = own[e]
        second[place, :, 384:512], second[place, :, 512:640] = made
        return carry

    in_halves(one, lambda h, at: pltpu.make_async_copy(out.at[at], windows.at[at, :, 384:], sems.at[h]))


def adjoint(f, gates, misfit, parts, window, lam, curl, x_masks):
    lam[:, FZ:, :] = jnp.zeros((3, 8, LANES), jnp.float32)
    curl[:, :8, :] = jnp.zeros((3, 8, LANES), jnp.float32)
    x_of = lax.broadcasted_iota(jnp.int32, (8, LANES), 1) % FP
    x_masks[0] = (x_of != FP - 1).astype(jnp.float32)
    x_masks[1] = (x_of != 0).astype(jnp.float32)
    times = 0.1 * jnp.exp((LN15 / (NTIMES - 1)) * gates[...].astype(jnp.float32))
    scaled = -LOG2E * times
    all_lanes = lax.broadcasted_iota(jnp.int32, (8, LANES), 1)
    last_y = all_lanes >= LANES - FP
    first_y = all_lanes < FP

    def ahead_x(v):
        return pltpu.roll(v, LANES - 1, 1) * x_masks[0]

    def behind_x(v):
        return pltpu.roll(v, 1, 1) * x_masks[1]

    def ahead_y(v):
        return jnp.where(last_y, 0.0, pltpu.roll(v, LANES - FP, 1))

    def behind_y(v):
        return jnp.where(first_y, 0.0, pltpu.roll(v, FP, 1))

    low = lane_iota(FZ) < 64
    for c in range(4):
        for q in range(4):
            window[c, :, 384 * q + 384 : 384 * q + 768] = parts[4 * c + q, :, :384].astype(jnp.float32)
        for base, p in ((0, 4 * c), (1920, 4 * c + 2)):
            head, rest = (parts[p, :, n : n + 128].astype(jnp.float32) for n in (384, 512))
            then, last = (turn(parts[p + 1, :, n : n + 128].astype(jnp.float32), 64) for n in (384, 512))
            window[c, :, base : base + 128] = head
            window[c, :, base + 128 : base + 256] = jnp.where(low, rest, then)
            window[c, :, base + 256 : base + 384] = jnp.where(low, then, last)
    residue = misfit[pl.ds(f, 1), :]
    t_of = [jnp.broadcast_to(scaled[:, g : g + 1], (8, 128)) for g in range(GATES)]
    r_of = [jnp.broadcast_to(residue[:, g : g + 1], (8, 128)) for g in range(GATES)]

    def weigh(i, carry):
        z = pl.ds(pl.multiple_of(8 * i, 8), 8)
        for c0 in range(0, LANES, 384):
            at = slice(c0, c0 + 384)
            sigma = window[3, z, at]
            weight = jnp.zeros_like(sigma)
            for g in range(GATES):
                t3 = jnp.concatenate([t_of[g]] * 3, 1)
                r3 = jnp.concatenate([r_of[g]] * 3, 1)
                weight = weight + r3 * jnp.exp2(sigma * t3)
            for c in range(3):
                lam[c, z, at] = weight * window[c, z, at]
        return carry

    lax.fori_loop(0, FZ // 8, weigh, 0)

    def step(n, carry):
        for i in range(FZ // 8):
            z = slice(8 * i, 8 * i + 8)
            up = slice(8 * i + 1, 8 * i + 9)
            vx, vy, vz = lam[0, z, :], lam[1, z, :], lam[2, z, :]
            at = slice(8 * i + 8, 8 * i + 16)
            curl[0, at, :] = (ahead_y(vz) - vz) - (lam[1, up, :] - vy)
            curl[1, at, :] = (lam[0, up, :] - vx) - (ahead_x(vz) - vz)
            curl[2, at, :] = (ahead_x(vy) - vy) - (ahead_y(vx) - vx)
        for i in range(FZ // 8):
            z = slice(8 * i, 8 * i + 8)
            at = slice(8 * i + 8, 8 * i + 16)
            down = slice(8 * i + 7, 8 * i + 15)
            wx, wy, wz = curl[0, at, :], curl[1, at, :], curl[2, at, :]
            ux = (curl[1, down, :] - wy) - (behind_y(wz) - wz)
            uy = (behind_x(wz) - wz) - (curl[0, down, :] - wx)
            uz = (behind_y(wx) - wx) - (behind_x(wy) - wy)
            sigma = window[3, z, :]
            for c, u in enumerate((ux, uy, uz)):
                v = lam[c, z, :]
                lam[c, z, :] = v - STEP * (u + sigma * v)
        return carry

    lax.fori_loop(0, STEPS, step, 0)


def solve_kernel(me, table, gates, misfit, parts, second, lam_out, back, window, lam, curl, local, x_masks):
    f, own = table[0, me[0]], table[2, me[0]]
    adjoint(f, gates, misfit, parts, window, lam, curl, x_masks)
    for i in range(FZ // 8):
        z = slice(8 * i, 8 * i + 8)
        total = None
        for c in range(3):
            v = lam[c, z, :]
            lam_out[c, z, :] = jnp.where(own == 1, v, 0.0)
            term = v * window[c, z, :]
            total = term if total is None else total + term
        local[z, :] = total
    lane = lane_iota(FZ)
    for j in range(N_DEV):

        def taken(base, high_at, rest_at):
            a, r = base // 128, base % 128
            both = [local[:, 128 * g : 128 * g + 128] for g in (a, min(a + 1, LANES // 128 - 1))]
            high = [v.astype(jnp.bfloat16).astype(jnp.float32) for v in both]
            rest = [turn(v - h, rest_at - r) for v, h in zip(both, high)]
            return [turn(h, high_at - r) for h in high], rest, 128 - r

        high, rest, edge = taken(384 + 96 * j, 64, 80)
        halo_high, halo_rest, halo_edge = taken(FP * (j if j < 8 else 32 + j), 32, 48)
        low = second[j, :, 512:640].astype(jnp.float32)
        v4 = jnp.where(lane < 64, low, jnp.where(lane - 64 < edge, high[0], high[1]))
        v5 = jnp.where(lane - 32 < halo_edge, halo_high[0], halo_high[1])
        v5 = jnp.where(lane < 32, jnp.where(lane + 64 < edge, high[0], high[1]), v5)
        v5 = jnp.where(lane < 80, v5, jnp.where(lane - 80 < edge, rest[0], rest[1]))
        v6 = jnp.where(lane - 48 < halo_edge, halo_rest[0], halo_rest[1])
        v6 = jnp.where(lane < 48, jnp.where(lane + 48 < edge, rest[0], rest[1]), v6)
        back[j, :, :512] = second[j, :, :512]
        for b, v in enumerate((v4, v5, v6)):
            back[j, :, 512 + 128 * b : 640 + 128 * b] = v.astype(jnp.bfloat16)


def second_kernel(me, table, gates, misfit, parts, own, adjoint_out, window, lam, curl, x_masks, sems):
    first = pltpu.make_async_copy(own, adjoint_out.at[0], sems.at[0])
    first.start()
    f = table[1, me[0]]

    @pl.when(f >= 0)
    def _():
        adjoint(f, gates, misfit, parts, window, lam, curl, x_masks)

    @pl.when(f < 0)
    def _():
        lam[:, :FZ, :] = jnp.zeros((3, FZ, LANES), jnp.float32)

    copy = pltpu.make_async_copy(lam.at[:, :FZ, :], adjoint_out.at[1], sems.at[1])
    copy.start()
    copy.wait()
    first.wait()


def regularize_kernel(conductivity, out):
    logs = jnp.log(conductivity[...].astype(jnp.float32))
    delta = logs[1:] - logs[:-1]
    zero_row = jnp.zeros_like(logs[:1])
    out[...] = jnp.concatenate([zero_row, delta], 0) - jnp.concatenate([delta, zero_row], 0)


def add_row(out, row, source, at, o):
    lane = lane_iota(FZ)
    g, s = o // 128, o % 128
    turned = turn(source, o - at)
    out[row, g] = out[row, g] + jnp.where((lane >= s) & (lane < s + FP), turned, 0.0)
    out[row, g + 1] = out[row, g + 1] + jnp.where(lane < s + FP - 128, turned, 0.0)


def scatter_halo_kernel(anchor, table, back, out, rows):
    rows[...] = jnp.zeros_like(rows)

    def one(e, carry):
        v5, v6 = (back[e, :, n : n + 128].astype(jnp.float32) for n in (640, 768))
        add_row(rows, 0, v5 + turn(v6, -16), 32, anchor[0, table[0, e]])
        return carry

    lax.fori_loop(0, N_DEV, one, 0, unroll=UNROLL)
    out[...] = rows[0, :4]


def scatter_own_kernel(anchor, table, back, out):
    out[...] = jnp.zeros_like(out)
    lane = lane_iota(FZ)

    def one(e, carry):
        o = anchor[0, table[0, e]]
        v4, v5, v6 = (back[e, :, 512 + 128 * b : 640 + 128 * b].astype(jnp.float32) for b in range(3))
        both = jnp.where(lane >= 64, v4, v5) + turn(jnp.where(lane >= 80, v5, v6), -16)
        add_row(out, 0, both, 64, o)
        add_row(out, 1, both, 112, o)
        return carry

    lax.fori_loop(0, N_DEV, one, 0, unroll=UNROLL)


def collect_kernel(own, halo, out):
    lane_row = lane_iota(32) // TX
    for g in range(4):
        whole = (own[0, g], own[1, g], halo[g])
        rows = [turn(v[:32], 32 * n) for n, v in enumerate(whole)]
        deep = jnp.concatenate([turn(v[32:], 96) for v in whole] + [jnp.zeros((8, 128), jnp.float32)], 0)
        for n in range(4):
            v = jnp.where(lane_row == n, rows[0], deep)
            for m in range(1, 3):
                v = jnp.where(lane_row == (n + m) % 4, rows[m], v)
            out[4 * g + n] = v


def join_kernel(me, sums, smooth, out):
    lane = lane_iota(FZ)
    base = TX * (me[0] % 4)
    made = []
    for v in range(8):
        halves = []
        for n in range(2):
            top = turn(sums[2 * v + n], 64 * n - base)
            even, odd = (turn(sums[2 * v + n, 8 * m : 8 * m + 8], 64 * n + 32 + 32 * m - base) for m in range(2))
            halves.append(jnp.concatenate([top, jnp.where(lane[:8] % 64 < TX, even, odd)], 0))
        made.append(jnp.where(lane < 64, halves[0], halves[1]))
    for j in range(N_DEV):
        v = (24 + j) // 4 if j < 8 else (j - 8) // 4
        at = TX * (j % 4) - base
        halo = jnp.concatenate([turn(sums[j], at - 64), turn(sums[j, 16:24], at - 96)], 0)
        made[v] = made[v] + jnp.where(lane // TX == j % 4, halo, 0.0)
    for v in range(8):
        at = slice(128 * v, 128 * v + 128)
        out[:FZ, at] = smooth[:FZ, at] + made[v]
    out[FZ:, :] = smooth[FZ:, :]


def to_neighbours(array, goes_up):
    bands, width = lax.axis_size("row"), lax.axis_size("dev")
    pairs = []
    for r in range(bands):
        for d in range(width):
            other = r + 1 if goes_up(d) else r - 1
            if 0 <= other < bands:
                pairs.append((r * width + d, other * width + d))
    return lax.ppermute(array, ("row", "dev"), pairs)


SMEM = pl.BlockSpec(memory_space=pltpu.SMEM)
VMEM = pl.BlockSpec(memory_space=pltpu.VMEM)
ANY = pl.BlockSpec(memory_space=pl.ANY)
PARAMS = pltpu.CompilerParams(vmem_limit_bytes=24 * 2**20)
F32 = jnp.float32
WIDE = 64 * 2**20 - 640 * 2**10
SMALL = pl.CostEstimate(flops=10**6, bytes_accessed=10**6, transcendentals=10**5)
WORK = [
    pltpu.VMEM((4, FZ, LANES), F32),
    pltpu.VMEM((3, FZ + 8, LANES), F32),
    pltpu.VMEM((3, FZ + 8, LANES), F32),
]
MASKS = pltpu.VMEM((2, 8, LANES), F32)


def exchange(blocks):
    return lax.all_to_all(blocks, "dev", 0, 0, tiled=True)


def per_device(primary, conductivity, anchor_x, owner, gate_index, misfit):
    me = lax.axis_index("dev").astype(jnp.int32).reshape(1)
    gates, residues = gate_index.reshape(1, GATES), misfit[0]
    spread = pl.pallas_call(
        tile_kernel,
        out_shape=jax.ShapeDtypeStruct((N_DEV, FZ, QIN), jnp.bfloat16),
        in_specs=[ANY, ANY],
        out_specs=ANY,
        scratch_shapes=[
            pltpu.VMEM((4, DEPTH, TX * TY), jnp.bfloat16),
            pltpu.VMEM((N_DEV, FZ, QIN), jnp.bfloat16),
            pltpu.SemaphoreType.DMA((2, 4)),
        ],
        compiler_params=pltpu.CompilerParams(vmem_limit_bytes=WIDE),
        name="tile",
    )(primary, conductivity)
    tiles = exchange(spread)
    halo_tiles = to_neighbours(tiles[:, :, 256:], lambda d: d % 4 < 2)
    cut_shape = jax.ShapeDtypeStruct((N_DEV, FZ, CUT), jnp.bfloat16)
    own_cut, windows, table = pl.pallas_call(
        cut_own_kernel,
        out_shape=(
            jax.ShapeDtypeStruct((N_DEV, FZ, 384), jnp.bfloat16),
            cut_shape,
            jax.ShapeDtypeStruct((3, N_DEV), jnp.int32),
        ),
        in_specs=[SMEM, SMEM, VMEM],
        out_specs=(VMEM, ANY, SMEM),
        scratch_shapes=[pltpu.SMEM((N_DEV + 1,), jnp.int32), pltpu.SemaphoreType.DMA((2,))],
        compiler_params=PARAMS,
        cost_estimate=SMALL,
        name="cut_own",
    )(anchor_x, owner, tiles)
    windows, second = pl.pallas_call(
        cut_halo_kernel,
        out_shape=(cut_shape, jax.ShapeDtypeStruct((N_DEV + 1, FZ, CUT), jnp.bfloat16)),
        in_specs=[SMEM, SMEM, SMEM, VMEM, VMEM, ANY],
        out_specs=(ANY, VMEM),
        scratch_shapes=[pltpu.VMEM((N_DEV, FZ, CUT - 384), jnp.bfloat16), pltpu.SemaphoreType.DMA((2,))],
        input_output_aliases={5: 0},
        compiler_params=PARAMS,
        name="cut_halo",
    )(anchor_x, owner, table, halo_tiles, own_cut, windows)
    windows, me = lax.optimization_barrier((windows, me))
    parts = exchange(windows)
    lam, back = pl.pallas_call(
        solve_kernel,
        out_shape=(
            jax.ShapeDtypeStruct((3, FZ, LANES), F32),
            jax.ShapeDtypeStruct((N_DEV, FZ, BACK), jnp.bfloat16),
        ),
        in_specs=[SMEM, SMEM, VMEM, VMEM, VMEM, VMEM],
        out_specs=(VMEM, VMEM),
        scratch_shapes=[*WORK, pltpu.VMEM((FZ, LANES), F32), MASKS],
        compiler_params=PARAMS,
        name="solve",
    )(me, table, gates, residues, parts, second)
    back = exchange(back)
    halo_rows = pl.pallas_call(
        scatter_halo_kernel,
        out_shape=jax.ShapeDtypeStruct((4, FZ, 128), F32),
        in_specs=[SMEM, SMEM, VMEM],
        out_specs=VMEM,
        scratch_shapes=[pltpu.VMEM((1, 5, FZ, 128), F32)],
        compiler_params=PARAMS,
        name="scatter_halo",
    )(anchor_x, table, back)
    halo_rows, sums = lax.optimization_barrier((halo_rows, back))
    halo_rows = to_neighbours(halo_rows, lambda d: d >= 8)
    own_rows = pl.pallas_call(
        scatter_own_kernel,
        out_shape=jax.ShapeDtypeStruct((2, 5, FZ, 128), F32),
        in_specs=[SMEM, SMEM, VMEM],
        out_specs=VMEM,
        compiler_params=PARAMS,
        cost_estimate=SMALL,
        name="scatter_own",
    )(anchor_x, table, sums)
    columns = pl.pallas_call(
        collect_kernel,
        out_shape=jax.ShapeDtypeStruct((N_DEV, 32, 128), F32),
        in_specs=[VMEM, VMEM],
        out_specs=VMEM,
        compiler_params=PARAMS,
        name="collect",
    )(own_rows, halo_rows)
    columns, back, layers = lax.optimization_barrier((columns, back, conductivity))
    smooth = pl.pallas_call(
        regularize_kernel,
        out_shape=jax.ShapeDtypeStruct(conductivity.shape, F32),
        in_specs=[VMEM],
        out_specs=VMEM,
        compiler_params=PARAMS,
        cost_estimate=SMALL,
        name="regularize",
    )(layers)
    adjoint_field = pl.pallas_call(
        second_kernel,
        out_shape=jax.ShapeDtypeStruct((MOST, 3, FZ, LANES), F32),
        in_specs=[SMEM, SMEM, VMEM, VMEM, VMEM, ANY],
        out_specs=ANY,
        scratch_shapes=[*WORK, MASKS, pltpu.SemaphoreType.DMA((2,))],
        compiler_params=PARAMS,
        cost_estimate=pl.CostEstimate(flops=2 * 10**7, bytes_accessed=4 * 10**6, transcendentals=3 * 10**6),
        name="second",
    )(me, table, gates, residues, back, lam)
    columns, adjoint_field = lax.optimization_barrier((exchange(columns), adjoint_field))
    gradient = pl.pallas_call(
        join_kernel,
        out_shape=jax.ShapeDtypeStruct(conductivity.shape, F32),
        in_specs=[SMEM, VMEM, VMEM],
        out_specs=VMEM,
        compiler_params=PARAMS,
        name="join",
    )(me, columns, smooth)
    return gradient, adjoint_field


def solution(mesh):
    in_specs = (
        P(None, None, ("row", "dev")),
        P(None, ("row", "dev")),
        P("row", None),
        P("row", None),
        P(),
        P("row", None, None),
    )
    out_specs = (P(None, ("row", "dev")), P(("row", "dev"), None, None, None))
    return jax.shard_map(
        per_device, mesh=mesh, in_specs=in_specs, out_specs=out_specs, check_vma=False
    )
```

```python
import jax
import jax.numpy as jnp
from jax import lax
from jax.experimental import pallas as pl
from jax.experimental.pallas import tpu as pltpu
from jax.sharding import PartitionSpec as P

TX = 32
TY = 32
FZ = 40
FP = 48
GATES = 30
NTIMES = 64
STEPS = 2
MOST = 2
FOOT_ROW = 16
N_DEV = 16
STEP = 0.05

LANES = FP * FP
OWN_ROWS = 8
QIN = 384
CUT = 640
BACK = 896
DEPTH = 48
UNROLL = 8
CUT_UNROLL = 8
LOG2E = 1.4426950408889634
LN15 = 2.70805020110221


def turn(v, by):
    return pltpu.roll(v, by % 128, 1)


def lane_iota(rows):
    return lax.broadcasted_iota(jnp.int32, (rows, 128), 1)


def tall(mask):
    return jnp.concatenate([mask] * (FZ // 8), 0)


def assign(owner, table, seconds):
    for e in range(N_DEV):
        table[0, e] = -1
        table[1, e] = -1
    for f in range(FOOT_ROW):
        e = owner[0, f]
        held, other = table[0, e], table[1, e]
        table[0, e] = jnp.where(held >= 0, held, f)
        table[1, e] = jnp.where(held >= 0, f, other)
    n = jnp.int32(0)
    for e in range(N_DEV):
        other = table[1, e]
        seconds[n] = other
        n = n + (other >= 0).astype(jnp.int32)
    n = jnp.int32(0)
    for e in range(N_DEV):
        held = table[0, e]
        table[2, e] = (held >= 0).astype(jnp.int32)
        table[0, e] = jnp.where(held >= 0, held, seconds[n])
        n = n + (held < 0).astype(jnp.int32)


def tile_kernel(primary, conductivity, out_to, held, out, sems):
    arrivals = [pltpu.make_async_copy(primary.at[c, :DEPTH], held.at[c], sems.at[0, c]) for c in range(3)]
    arrivals.append(pltpu.make_async_copy(conductivity.at[:DEPTH], held.at[3], sems.at[0, 3]))
    for copy in arrivals:
        copy.start()
    leaving = []
    for c in range(4):
        arrivals[c].wait()
        for q, start in enumerate((768, 896, 0, 128)):
            out[4 * c + q, :, :256] = held[c, :FZ, 256 * q : 256 * q + 256]
            out[4 * c + q, :, 256:] = held[c, :FZ, start : start + 128]
        some = slice(4 * c, 4 * c + 4)
        leaving.append(pltpu.make_async_copy(out.at[some], out_to.at[some], sems.at[1, c]))
        leaving[-1].start()
    for copy in leaving:
        copy.wait()


def cut_rows(tiles, o, count):
    d0, s = o // TX, o % TX
    row_in = lane_iota(8) // TX
    made, codes = [], []
    for v in range(-(-FP * count // 128)):
        at = lane_iota(8) + 128 * v
        y = sum((at >= FP * j).astype(jnp.int32) for j in range(1, count + 1))
        codes.append(8 * (y // 4) + y % 4 + 2 * lax.shift_right_logical(at - FP * y + s, 5))
        made.append(jnp.zeros((FZ, 128), jnp.float32))
    for m in range(count // 4):
        tile = [tiles(jnp.minimum(d0 + t, N_DEV - 1), m).astype(jnp.float32) for t in range(3)]
        for n in range(8):
            from_t = [t for t in range(3) if 0 <= n - 2 * t < 4]
            src = tile[from_t[0]]
            for t in from_t[1:]:
                src = jnp.where(tall(row_in == n - 2 * t), tile[t], src)
            turned = turn(src, 192 * m + 16 * n - s)
            rows = [(192 * m + FP * (n - 2 * t), t) for t in from_t]
            for v in range(len(made)):
                if any(
                    at + max(0, TX * t - 31) < 128 * (v + 1) and at + min(FP, TX * (t + 1)) > 128 * v for at, t in rows
                ):
                    made[v] = jnp.where(tall(codes[v] == 8 * m + n), turned, made[v])
    return [v.astype(jnp.bfloat16) for v in made]


def in_halves(one, copy_of):
    half = N_DEV // 2
    copies = [copy_of(h, slice(half * h, half * h + half)) for h in range(2)]
    for h, copy in enumerate(copies):
        lax.fori_loop(half * h, half * h + half, one, 0, unroll=CUT_UNROLL)
        copy.start()
    for copy in copies:
        copy.wait()


def cut_own_kernel(anchor, owner, tiles, out, windows, table, seconds, sems):
    assign(owner, table, seconds)

    def one(e, carry):
        o = anchor[0, table[0, e]]
        made = cut_rows(lambda d, m: tiles[d, :, 128 * m : 128 * m + 128], o, OWN_ROWS)
        for v, lanes in enumerate(made):
            out[e, :, 128 * v : 128 * v + 128] = lanes
        return carry

    in_halves(one, lambda h, at: pltpu.make_async_copy(out.at[at], windows.at[at, :, :384], sems.at[h]))


def cut_halo_kernel(anchor, owner, table, tiles, own, windows_in, windows, second, out, sems):
    del windows_in

    def one(e, carry):
        f = table[0, e]
        w = owner[0, f]
        made = cut_rows(lambda d, m: tiles[d], anchor[0, f], 4)
        out[e, :, :128], out[e, :, 128:] = made
        place = jnp.where(table[1, w] == f, w, N_DEV)
        second[place, :, :384] = own[e]
        second[place, :, 384:512], second[place, :, 512:640] = made
        return carry

    in_halves(one, lambda h, at: pltpu.make_async_copy(out.at[at], windows.at[at, :, 384:], sems.at[h]))


def adjoint(f, gates, misfit, parts, window, lam, curl, x_masks):
    lam[:, FZ:, :] = jnp.zeros((3, 8, LANES), jnp.float32)
    curl[:, :8, :] = jnp.zeros((3, 8, LANES), jnp.float32)
    x_of = lax.broadcasted_iota(jnp.int32, (8, LANES), 1) % FP
    x_masks[0] = (x_of != FP - 1).astype(jnp.float32)
    x_masks[1] = (x_of != 0).astype(jnp.float32)
    times = 0.1 * jnp.exp((LN15 / (NTIMES - 1)) * gates[...].astype(jnp.float32))
    scaled = -LOG2E * times
    all_lanes = lax.broadcasted_iota(jnp.int32, (8, LANES), 1)
    last_y = all_lanes >= LANES - FP
    first_y = all_lanes < FP

    def ahead_x(v):
        return pltpu.roll(v, LANES - 1, 1) * x_masks[0]

    def behind_x(v):
        return pltpu.roll(v, 1, 1) * x_masks[1]

    def ahead_y(v):
        return jnp.where(last_y, 0.0, pltpu.roll(v, LANES - FP, 1))

    def behind_y(v):
        return jnp.where(first_y, 0.0, pltpu.roll(v, FP, 1))

    low = lane_iota(FZ) < 64
    for c in range(4):
        for q in range(4):
            window[c, :, 384 * q + 384 : 384 * q + 768] = parts[4 * c + q, :, :384].astype(jnp.float32)
        for base, p in ((0, 4 * c), (1920, 4 * c + 2)):
            head, rest = (parts[p, :, n : n + 128].astype(jnp.float32) for n in (384, 512))
            then, last = (turn(parts[p + 1, :, n : n + 128].astype(jnp.float32), 64) for n in (384, 512))
            window[c, :, base : base + 128] = head
            window[c, :, base + 128 : base + 256] = jnp.where(low, rest, then)
            window[c, :, base + 256 : base + 384] = jnp.where(low, then, last)
    residue = misfit[pl.ds(f, 1), :]
    t_of = [jnp.broadcast_to(scaled[:, g : g + 1], (8, 128)) for g in range(GATES)]
    r_of = [jnp.broadcast_to(residue[:, g : g + 1], (8, 128)) for g in range(GATES)]

    def weigh(i, carry):
        z = pl.ds(pl.multiple_of(8 * i, 8), 8)
        for c0 in range(0, LANES, 384):
            at = slice(c0, c0 + 384)
            sigma = window[3, z, at]
            weight = jnp.zeros_like(sigma)
            for g in range(GATES):
                t3 = jnp.concatenate([t_of[g]] * 3, 1)
                r3 = jnp.concatenate([r_of[g]] * 3, 1)
                weight = weight + r3 * jnp.exp2(sigma * t3)
            for c in range(3):
                lam[c, z, at] = weight * window[c, z, at]
        return carry

    lax.fori_loop(0, FZ // 8, weigh, 0)

    def step(n, carry):
        for i in range(FZ // 8):
            z = slice(8 * i, 8 * i + 8)
            up = slice(8 * i + 1, 8 * i + 9)
            vx, vy, vz = lam[0, z, :], lam[1, z, :], lam[2, z, :]
            at = slice(8 * i + 8, 8 * i + 16)
            curl[0, at, :] = (ahead_y(vz) - vz) - (lam[1, up, :] - vy)
            curl[1, at, :] = (lam[0, up, :] - vx) - (ahead_x(vz) - vz)
            curl[2, at, :] = (ahead_x(vy) - vy) - (ahead_y(vx) - vx)
        for i in range(FZ // 8):
            z = slice(8 * i, 8 * i + 8)
            at = slice(8 * i + 8, 8 * i + 16)
            down = slice(8 * i + 7, 8 * i + 15)
            wx, wy, wz = curl[0, at, :], curl[1, at, :], curl[2, at, :]
            ux = (curl[1, down, :] - wy) - (behind_y(wz) - wz)
            uy = (behind_x(wz) - wz) - (curl[0, down, :] - wx)
            uz = (behind_y(wx) - wx) - (behind_x(wy) - wy)
            sigma = window[3, z, :]
            for c, u in enumerate((ux, uy, uz)):
                v = lam[c, z, :]
                lam[c, z, :] = v - STEP * (u + sigma * v)
        return carry

    lax.fori_loop(0, STEPS, step, 0)


def solve_kernel(me, table, gates, misfit, parts, second, lam_out, back, window, lam, curl, local, x_masks):
    f, own = table[0, me[0]], table[2, me[0]]
    adjoint(f, gates, misfit, parts, window, lam, curl, x_masks)
    for i in range(FZ // 8):
        z = slice(8 * i, 8 * i + 8)
        total = None
        for c in range(3):
            v = lam[c, z, :]
            lam_out[c, z, :] = jnp.where(own == 1, v, 0.0)
            term = v * window[c, z, :]
            total = term if total is None else total + term
        local[z, :] = total
    lane = lane_iota(FZ)
    for j in range(N_DEV):

        def taken(base, high_at, rest_at):
            a, r = base // 128, base % 128
            both = [local[:, 128 * g : 128 * g + 128] for g in (a, min(a + 1, LANES // 128 - 1))]
            high = [v.astype(jnp.bfloat16).astype(jnp.float32) for v in both]
            rest = [turn(v - h, rest_at - r) for v, h in zip(both, high)]
            return [turn(h, high_at - r) for h in high], rest, 128 - r

        high, rest, edge = taken(384 + 96 * j, 64, 80)
        halo_high, halo_rest, halo_edge = taken(FP * (j if j < 8 else 32 + j), 32, 48)
        low = second[j, :, 512:640].astype(jnp.float32)
        v4 = jnp.where(lane < 64, low, jnp.where(lane - 64 < edge, high[0], high[1]))
        v5 = jnp.where(lane - 32 < halo_edge, halo_high[0], halo_high[1])
        v5 = jnp.where(lane < 32, jnp.where(lane + 64 < edge, high[0], high[1]), v5)
        v5 = jnp.where(lane < 80, v5, jnp.where(lane - 80 < edge, rest[0], rest[1]))
        v6 = jnp.where(lane - 48 < halo_edge, halo_rest[0], halo_rest[1])
        v6 = jnp.where(lane < 48, jnp.where(lane + 48 < edge, rest[0], rest[1]), v6)
        back[j, :, :512] = second[j, :, :512]
        for b, v in enumerate((v4, v5, v6)):
            back[j, :, 512 + 128 * b : 640 + 128 * b] = v.astype(jnp.bfloat16)


def second_kernel(me, table, gates, misfit, parts, own, adjoint_out, window, lam, curl, x_masks, sems):
    first = pltpu.make_async_copy(own, adjoint_out.at[0], sems.at[0])
    first.start()
    f = table[1, me[0]]

    @pl.when(f >= 0)
    def _():
        adjoint(f, gates, misfit, parts, window, lam, curl, x_masks)

    @pl.when(f < 0)
    def _():
        lam[:, :FZ, :] = jnp.zeros((3, FZ, LANES), jnp.float32)

    copy = pltpu.make_async_copy(lam.at[:, :FZ, :], adjoint_out.at[1], sems.at[1])
    copy.start()
    copy.wait()
    first.wait()


def regularize_kernel(conductivity, out):
    logs = jnp.log(conductivity[...].astype(jnp.float32))
    delta = logs[1:] - logs[:-1]
    zero_row = jnp.zeros_like(logs[:1])
    out[...] = jnp.concatenate([zero_row, delta], 0) - jnp.concatenate([delta, zero_row], 0)


def add_row(out, row, source, at, o):
    lane = lane_iota(FZ)
    g, s = o // 128, o % 128
    turned = turn(source, o - at)
    out[row, g] = out[row, g] + jnp.where((lane >= s) & (lane < s + FP), turned, 0.0)
    out[row, g + 1] = out[row, g + 1] + jnp.where(lane < s + FP - 128, turned, 0.0)


def scatter_halo_kernel(anchor, table, back, out, rows):
    rows[...] = jnp.zeros_like(rows)

    def one(e, carry):
        v5, v6 = (back[e, :, n : n + 128].astype(jnp.float32) for n in (640, 768))
        add_row(rows, 0, v5 + turn(v6, -16), 32, anchor[0, table[0, e]])
        return carry

    lax.fori_loop(0, N_DEV, one, 0, unroll=UNROLL)
    out[...] = rows[0, :4]


def scatter_own_kernel(anchor, table, back, out):
    out[...] = jnp.zeros_like(out)
    lane = lane_iota(FZ)

    def one(e, carry):
        o = anchor[0, table[0, e]]
        v4, v5, v6 = (back[e, :, 512 + 128 * b : 640 + 128 * b].astype(jnp.float32) for b in range(3))
        both = jnp.where(lane >= 64, v4, v5) + turn(jnp.where(lane >= 80, v5, v6), -16)
        add_row(out, 0, both, 64, o)
        add_row(out, 1, both, 112, o)
        return carry

    lax.fori_loop(0, N_DEV, one, 0, unroll=UNROLL)


def collect_kernel(own, halo, out):
    lane_row = lane_iota(32) // TX
    for g in range(4):
        whole = (own[0, g], own[1, g], halo[g])
        rows = [turn(v[:32], 32 * n) for n, v in enumerate(whole)]
        deep = jnp.concatenate([turn(v[32:], 96) for v in whole] + [jnp.zeros((8, 128), jnp.float32)], 0)
        for n in range(4):
            v = jnp.where(lane_row == n, rows[0], deep)
            for m in range(1, 3):
                v = jnp.where(lane_row == (n + m) % 4, rows[m], v)
            out[4 * g + n] = v


def join_kernel(me, sums, smooth, out_to, out, sems):
    deep = pltpu.make_async_copy(smooth.at[FZ:, :], out_to.at[FZ:, :], sems.at[0])
    deep.start()
    copies = [deep]
    lane = lane_iota(FZ)
    base = TX * (me[0] % 4)
    for order, (first, last) in enumerate(((2, 6), (0, 2), (6, 8))):
        for v in range(first, last):
            halves = []
            for n in range(2):
                top = turn(sums[2 * v + n], 64 * n - base)
                even, odd = (turn(sums[2 * v + n, 8 * m : 8 * m + 8], 64 * n + 32 + 32 * m - base) for m in range(2))
                halves.append(jnp.concatenate([top, jnp.where(lane[:8] % 64 < TX, even, odd)], 0))
            made = jnp.where(lane < 64, halves[0], halves[1])
            for j in range(N_DEV):
                if v == ((24 + j) // 4 if j < 8 else (j - 8) // 4):
                    at = TX * (j % 4) - base
                    halo = jnp.concatenate([turn(sums[j], at - 64), turn(sums[j, 16:24], at - 96)], 0)
                    made = made + jnp.where(lane // TX == j % 4, halo, 0.0)
            lanes = slice(128 * v, 128 * v + 128)
            out[:, lanes] = smooth[:FZ, lanes] + made
        lanes = slice(128 * first, 128 * last)
        copies.append(pltpu.make_async_copy(out.at[:, lanes], out_to.at[:FZ, lanes], sems.at[1 + order]))
        copies[-1].start()
    for copy in copies:
        copy.wait()


def to_neighbours(array, goes_up):
    bands, width = lax.axis_size("row"), lax.axis_size("dev")
    pairs = []
    for r in range(bands):
        for d in range(width):
            other = r + 1 if goes_up(d) else r - 1
            if 0 <= other < bands:
                pairs.append((r * width + d, other * width + d))
    return lax.ppermute(array, ("row", "dev"), pairs)


SMEM = pl.BlockSpec(memory_space=pltpu.SMEM)
VMEM = pl.BlockSpec(memory_space=pltpu.VMEM)
ANY = pl.BlockSpec(memory_space=pl.ANY)
PARAMS = pltpu.CompilerParams(vmem_limit_bytes=24 * 2**20)
F32 = jnp.float32
WIDE = 64 * 2**20 - 640 * 2**10
SMALL = pl.CostEstimate(flops=10**6, bytes_accessed=10**6, transcendentals=10**5)
WORK = [
    pltpu.VMEM((4, FZ, LANES), F32),
    pltpu.VMEM((3, FZ + 8, LANES), F32),
    pltpu.VMEM((3, FZ + 8, LANES), F32),
]
MASKS = pltpu.VMEM((2, 8, LANES), F32)


def exchange(blocks):
    return lax.all_to_all(blocks, "dev", 0, 0, tiled=True)


def per_device(primary, conductivity, anchor_x, owner, gate_index, misfit):
    me = lax.axis_index("dev").astype(jnp.int32).reshape(1)
    gates, residues = gate_index.reshape(1, GATES), misfit[0]
    spread = pl.pallas_call(
        tile_kernel,
        out_shape=jax.ShapeDtypeStruct((N_DEV, FZ, QIN), jnp.bfloat16),
        in_specs=[ANY, ANY],
        out_specs=ANY,
        scratch_shapes=[
            pltpu.VMEM((4, DEPTH, TX * TY), jnp.bfloat16),
            pltpu.VMEM((N_DEV, FZ, QIN), jnp.bfloat16),
            pltpu.SemaphoreType.DMA((2, 4)),
        ],
        compiler_params=pltpu.CompilerParams(vmem_limit_bytes=WIDE),
        name="tile",
    )(primary, conductivity)
    tiles = exchange(spread)
    halo_tiles = to_neighbours(tiles[:, :, 256:], lambda d: d % 4 < 2)
    cut_shape = jax.ShapeDtypeStruct((N_DEV, FZ, CUT), jnp.bfloat16)
    own_cut, windows, table = pl.pallas_call(
        cut_own_kernel,
        out_shape=(
            jax.ShapeDtypeStruct((N_DEV, FZ, 384), jnp.bfloat16),
            cut_shape,
            jax.ShapeDtypeStruct((3, N_DEV), jnp.int32),
        ),
        in_specs=[SMEM, SMEM, VMEM],
        out_specs=(VMEM, ANY, SMEM),
        scratch_shapes=[pltpu.SMEM((N_DEV + 1,), jnp.int32), pltpu.SemaphoreType.DMA((2,))],
        compiler_params=PARAMS,
        cost_estimate=SMALL,
        name="cut_own",
    )(anchor_x, owner, tiles)
    windows, second = pl.pallas_call(
        cut_halo_kernel,
        out_shape=(cut_shape, jax.ShapeDtypeStruct((N_DEV + 1, FZ, CUT), jnp.bfloat16)),
        in_specs=[SMEM, SMEM, SMEM, VMEM, VMEM, ANY],
        out_specs=(ANY, VMEM),
        scratch_shapes=[pltpu.VMEM((N_DEV, FZ, CUT - 384), jnp.bfloat16), pltpu.SemaphoreType.DMA((2,))],
        input_output_aliases={5: 0},
        compiler_params=PARAMS,
        name="cut_halo",
    )(anchor_x, owner, table, halo_tiles, own_cut, windows)
    windows, me = lax.optimization_barrier((windows, me))
    parts = exchange(windows)
    lam, back = pl.pallas_call(
        solve_kernel,
        out_shape=(
            jax.ShapeDtypeStruct((3, FZ, LANES), F32),
            jax.ShapeDtypeStruct((N_DEV, FZ, BACK), jnp.bfloat16),
        ),
        in_specs=[SMEM, SMEM, VMEM, VMEM, VMEM, VMEM],
        out_specs=(VMEM, VMEM),
        scratch_shapes=[*WORK, pltpu.VMEM((FZ, LANES), F32), MASKS],
        compiler_params=PARAMS,
        name="solve",
    )(me, table, gates, residues, parts, second)
    back = exchange(back)
    halo_rows = pl.pallas_call(
        scatter_halo_kernel,
        out_shape=jax.ShapeDtypeStruct((4, FZ, 128), F32),
        in_specs=[SMEM, SMEM, VMEM],
        out_specs=VMEM,
        scratch_shapes=[pltpu.VMEM((1, 5, FZ, 128), F32)],
        compiler_params=PARAMS,
        name="scatter_halo",
    )(anchor_x, table, back)
    halo_rows, sums = lax.optimization_barrier((halo_rows, back))
    halo_rows = to_neighbours(halo_rows, lambda d: d >= 8)
    own_rows = pl.pallas_call(
        scatter_own_kernel,
        out_shape=jax.ShapeDtypeStruct((2, 5, FZ, 128), F32),
        in_specs=[SMEM, SMEM, VMEM],
        out_specs=VMEM,
        compiler_params=PARAMS,
        cost_estimate=SMALL,
        name="scatter_own",
    )(anchor_x, table, sums)
    columns = pl.pallas_call(
        collect_kernel,
        out_shape=jax.ShapeDtypeStruct((N_DEV, 32, 128), F32),
        in_specs=[VMEM, VMEM],
        out_specs=VMEM,
        compiler_params=PARAMS,
        name="collect",
    )(own_rows, halo_rows)
    columns, back, layers = lax.optimization_barrier((columns, back, conductivity))
    smooth = pl.pallas_call(
        regularize_kernel,
        out_shape=jax.ShapeDtypeStruct(conductivity.shape, F32),
        in_specs=[VMEM],
        out_specs=VMEM,
        compiler_params=PARAMS,
        cost_estimate=SMALL,
        name="regularize",
    )(layers)
    adjoint_field = pl.pallas_call(
        second_kernel,
        out_shape=jax.ShapeDtypeStruct((MOST, 3, FZ, LANES), F32),
        in_specs=[SMEM, SMEM, VMEM, VMEM, VMEM, ANY],
        out_specs=ANY,
        scratch_shapes=[*WORK, MASKS, pltpu.SemaphoreType.DMA((2,))],
        compiler_params=PARAMS,
        cost_estimate=pl.CostEstimate(flops=2 * 10**7, bytes_accessed=4 * 10**6, transcendentals=3 * 10**6),
        name="second",
    )(me, table, gates, residues, back, lam)
    columns, adjoint_field = lax.optimization_barrier((exchange(columns), adjoint_field))
    gradient = pl.pallas_call(
        join_kernel,
        out_shape=jax.ShapeDtypeStruct(conductivity.shape, F32),
        in_specs=[SMEM, VMEM, VMEM],
        out_specs=ANY,
        scratch_shapes=[pltpu.VMEM((FZ, TX * TY), F32), pltpu.SemaphoreType.DMA((4,))],
        compiler_params=PARAMS,
        name="join",
    )(me, columns, smooth)
    return gradient, adjoint_field


def solution(mesh):
    in_specs = (
        P(None, None, ("row", "dev")),
        P(None, ("row", "dev")),
        P("row", None),
        P("row", None),
        P(),
        P("row", None, None),
    )
    out_specs = (P(None, ("row", "dev")), P(("row", "dev"), None, None, None))
    return jax.shard_map(
        per_device, mesh=mesh, in_specs=in_specs, out_specs=out_specs, check_vma=False
    )
```
